32 devices in a mesh: row: 2 (over x), col: 16 (over z, y, core).
Axes of the slice: x: 2, y: 2, z: 4, core: 2. Of those that a mesh axis runs over, the one named last changes fastest.
Arguments:
- tokens: bfloat16 [160, 8192], P('col', 'row'), may hold values from -6 to 6
- cotangent: bfloat16 [160, 8192], P('col', 'row'), may hold values from -6 to 6
- gate_tiles: bfloat16 [12, 2048, 128], P('row', 'col'), may hold values from -0.125 to 0.125
- up_tiles: bfloat16 [12, 2048, 128], P('row', 'col'), may hold values from -0.125 to 0.125
- down_tiles: bfloat16 [12, 2048, 128], P('row', 'col'), may hold values from -0.09375 to 0.09375
- tile_index: int32 [3, 12, 32], P(None, 'row', 'col'), may hold values from 0 to 31, as said below
- tile_counts: int32 [3, 2, 16], P(None, 'row', 'col'), may hold values from 1 to 6, as said below
Outputs:
- output: bfloat16 [160, 8192], P('col', 'row')
- input_grad: bfloat16 [160, 8192], P('col', 'row')
- gate_grad: float32 [12, 2048, 128], P('row', 'col')
- up_grad: float32 [12, 2048, 128], P('row', 'col')
- down_grad: float32 [12, 2048, 128], P('row', 'col')
The draws below stay inside these ranges and needn't reach their ends.
Inputs may be any that keep to these rules, and one draw needn't show every extreme that they name: `tile_index`: within one matrix, row group and column group, the 6 slots name distinct block pairs; for gate and up the row block is below 32 and the column block below 8, for down the row block is below 8 and the column block below 32. `tile_counts`: for each matrix some row group and column group has all 6 slots live.
All inputs are finite; a program needn't handle non-finite values.
Results may differ from the reference program's by a relative error of at most 0.0049.
Values may be sent and summed in bfloat16 or wider, within the bound.
A program may use at most 64 MiB of HBM per device.

```python
import jax
import jax.numpy as jnp

D = 8192
FF = 16384
TB = 128
CAP = 6
ROW_GROUPS = 2
COL_GROUPS = 16
TOKENS = 160
RB = 32
CB = 8
SLOTS = 12
TILE_COLS = 2048


def first_slots(one_key):
    return jax.random.permutation(one_key, RB * CB)[:CAP]


def draw_tile_index(key, part):
    group_total = 3 * ROW_GROUPS * COL_GROUPS
    key_list = jax.random.split(jax.random.fold_in(key, 17), group_total)
    chosen = jax.vmap(first_slots)(key_list).reshape(3, ROW_GROUPS, COL_GROUPS, CAP)
    down_pick = (jnp.arange(3) == 2)[:, None, None, None]
    row_blocks = jnp.where(down_pick, chosen // RB, chosen // CB)
    col_blocks = jnp.where(down_pick, chosen % RB, chosen % CB)
    pair_list = jnp.stack([row_blocks, col_blocks], axis=-1)
    pair_list = pair_list.transpose(0, 1, 3, 2, 4).reshape(3, ROW_GROUPS * CAP, COL_GROUPS * 2)
    return pair_list.astype(jnp.int32)


def draw_tile_counts(key, part):
    key_base, key_heavy, key_forced = jax.random.split(jax.random.fold_in(key, 29), 3)
    grid_shape = (3, ROW_GROUPS, COL_GROUPS)
    base_counts = jax.random.randint(key_base, grid_shape, 1, 4)
    heavy_mask = jax.random.randint(key_heavy, grid_shape, 0, 16) == 0
    counts = jnp.where(heavy_mask, CAP, base_counts).reshape(3, ROW_GROUPS * COL_GROUPS)
    forced = jax.random.randint(key_forced, (3,), 0, ROW_GROUPS * COL_GROUPS)
    counts = counts.at[jnp.arange(3), forced].set(CAP)
    return counts.reshape(grid_shape).astype(jnp.int32)


def steps_of(rng, dims, shards, least, largest):
    loudness, own = 1.0, jax.random.fold_in(rng, 6)
    for position, blocks in shards:
        steps = jnp.exp(jax.random.uniform(jax.random.fold_in(own, position), (blocks,), jnp.float32, least / len(shards), largest / len(shards)))
        loudness = loudness * jnp.repeat(steps, dims[position] // blocks).reshape([-1 if axis == position else 1 for axis in range(len(dims))])
    return loudness


def noise(key, dims, spread, most, cuts=(), kind=jnp.bfloat16):
    entries = spread * jax.random.normal(key, dims, jnp.float32)
    if cuts:
        entries = entries * steps_of(key, dims, cuts, -0.22, 0.18)
    return jnp.clip(entries, -most, most).astype(kind)


def setup_inputs(seed: int = 0) -> dict:
    splits = jax.random.split(jax.random.key(seed), 8)
    tokens = noise(splits[0], (TOKENS, D), 1.0, 6.0, ((0, 16), (1, 2)))
    cotangent = noise(splits[1], (TOKENS, D), 1.0, 6.0, ((0, 16), (1, 2)))
    gate_tiles = noise(splits[2], (SLOTS, TILE_COLS, TB), (D // 4) ** -0.5, 0.125, ((0, 2), (1, 16)))
    up_tiles = noise(splits[3], (SLOTS, TILE_COLS, TB), (D // 4) ** -0.5, 0.125, ((0, 2), (1, 16)))
    down_tiles = noise(splits[4], (SLOTS, TILE_COLS, TB), (FF // 4) ** -0.5, 0.09375, ((0, 2), (1, 16)))
    tile_index = draw_tile_index(jax.random.fold_in(splits[7], 71), 0)
    tile_counts = draw_tile_counts(jax.random.fold_in(splits[7], 71), 0)
    return dict(tokens=tokens, cotangent=cotangent, gate_tiles=gate_tiles, up_tiles=up_tiles, down_tiles=down_tiles, tile_index=tile_index, tile_counts=tile_counts)


def place_tiles(tiles, index, counts, row_count, col_count, is_down):
    tile_size = TB
    slot_count = CAP
    row_groups, col_groups = counts.shape
    blocks = tiles.reshape(row_groups, slot_count, col_groups, tile_size, tile_size).transpose(0, 2, 1, 3, 4)
    pair_list = index.reshape(row_groups, slot_count, col_groups, 2).transpose(0, 2, 1, 3)
    live_mask = jnp.arange(slot_count).astype(jnp.int32)[None, None, :] < counts[:, :, None]
    blocks = jnp.where(live_mask[..., None, None], blocks, jnp.zeros_like(blocks))
    row_group_ids = jnp.arange(row_groups).astype(jnp.int32)[:, None, None]
    col_group_ids = jnp.arange(col_groups).astype(jnp.int32)[None, :, None]
    if is_down:
        grid_rows = (col_group_ids * row_count + pair_list[..., 0]).astype(jnp.int32)
        grid_cols = (row_group_ids * col_count + pair_list[..., 1]).astype(jnp.int32)
        total_rows = col_groups * row_count
        total_cols = row_groups * col_count
    else:
        grid_rows = (row_group_ids * row_count + pair_list[..., 0]).astype(jnp.int32)
        grid_cols = (col_group_ids * col_count + pair_list[..., 1]).astype(jnp.int32)
        total_rows = row_groups * row_count
        total_cols = col_groups * col_count
    grid = jnp.zeros((total_rows, total_cols, tile_size, tile_size), tiles.dtype)
    grid = grid.at[grid_rows, grid_cols].add(blocks)
    dense = grid.transpose(0, 2, 1, 3).reshape(total_rows * tile_size, total_cols * tile_size)
    return dense, grid_rows, grid_cols, live_mask


def extract_tiles(full, grid_rows, grid_cols, live_mask):
    tile_size = TB
    total_rows = full.shape[0] // tile_size
    total_cols = full.shape[1] // tile_size
    grid = full.reshape(total_rows, tile_size, total_cols, tile_size).transpose(0, 2, 1, 3)
    chosen = grid[grid_rows, grid_cols]
    chosen = jnp.where(live_mask[..., None, None], chosen, jnp.zeros_like(chosen))
    row_groups, col_groups, slot_count = live_mask.shape
    return chosen.transpose(0, 2, 1, 3, 4).reshape(row_groups * slot_count, col_groups * tile_size, tile_size)


def reference(tokens, cotangent, gate_tiles, up_tiles, down_tiles, tile_index, tile_counts):
    w_gate, gate_rows, gate_cols, gate_live = place_tiles(gate_tiles, tile_index[0], tile_counts[0], RB, CB, False)
    w_up, up_rows, up_cols, up_live = place_tiles(up_tiles, tile_index[1], tile_counts[1], RB, CB, False)
    w_down, down_rows, down_cols, down_live = place_tiles(down_tiles, tile_index[2], tile_counts[2], CB, RB, True)
    gate_sum = jnp.dot(tokens, w_gate, preferred_element_type=jnp.float32)
    up_sum = jnp.dot(tokens, w_up, preferred_element_type=jnp.float32)
    sigmoid_gate = jax.nn.sigmoid(gate_sum)
    active = gate_sum * sigmoid_gate
    hidden = (active * up_sum).astype(jnp.bfloat16)
    output = jnp.dot(hidden, w_down, preferred_element_type=jnp.float32).astype(jnp.bfloat16)
    hidden_grad = jnp.dot(cotangent, w_down.T, preferred_element_type=jnp.float32)
    gate_act = (hidden_grad * up_sum * sigmoid_gate * (1.0 + gate_sum * (1.0 - sigmoid_gate))).astype(jnp.bfloat16)
    up_act = (hidden_grad * active).astype(jnp.bfloat16)
    input_sum = jnp.dot(gate_act, w_gate.T, preferred_element_type=jnp.float32) + jnp.dot(up_act, w_up.T, preferred_element_type=jnp.float32)
    input_grad = input_sum.astype(jnp.bfloat16)
    gate_grad = extract_tiles(jnp.dot(tokens.T, gate_act, preferred_element_type=jnp.float32), gate_rows, gate_cols, gate_live)
    up_grad = extract_tiles(jnp.dot(tokens.T, up_act, preferred_element_type=jnp.float32), up_rows, up_cols, up_live)
    down_grad = extract_tiles(jnp.dot(hidden.T, cotangent, preferred_element_type=jnp.float32), down_rows, down_cols, down_live)
    return (output, input_grad, gate_grad, up_grad, down_grad)
```

```python
import functools

import jax
import jax.numpy as jnp
from jax import lax
from jax.experimental import pallas as pl
from jax.experimental.pallas import tpu as pltpu
from jax.sharding import PartitionSpec as P

FF = 16384


def pick_blocks(data_rows, block_ids, tile_size):
    token_count = data_rows.shape[0]
    block_count = data_rows.shape[1] // tile_size
    split_rows = data_rows.reshape(token_count, block_count, tile_size)
    select = (block_ids[:, None] == jnp.arange(block_count)[None, :]).astype(jnp.bfloat16)
    picked = jnp.einsum("tbk,sb->tsk", split_rows, select, preferred_element_type=jnp.float32)
    return picked.astype(jnp.bfloat16)


def place_blocks(products, block_ids, live_mask, block_count):
    select = ((block_ids[:, None] == jnp.arange(block_count)[None, :]) & live_mask[:, None]).astype(
        jnp.float32
    )
    placed = jnp.einsum("tsn,sc->tcn", products, select, precision=lax.Precision.HIGHEST)
    return placed.reshape(products.shape[0], block_count * products.shape[2])


def sparse_apply(data_rows, tiles, in_ids, out_ids, live_mask, out_count):
    picked = pick_blocks(data_rows, in_ids, tiles.shape[-1])
    products = jnp.einsum("tsk,skn->tsn", picked, tiles, preferred_element_type=jnp.float32)
    return place_blocks(products, out_ids, live_mask, out_count)


def sparse_apply_back(data_rows, tiles, in_ids, out_ids, live_mask, out_count):
    picked = pick_blocks(data_rows, in_ids, tiles.shape[-1])
    products = jnp.einsum("tsn,skn->tsk", picked, tiles, preferred_element_type=jnp.float32)
    return place_blocks(products, out_ids, live_mask, out_count)


def tile_grads(left_rows, right_rows, left_ids, right_ids, live_mask, tile_size):
    left_picked = pick_blocks(left_rows, left_ids, tile_size)
    right_picked = pick_blocks(right_rows, right_ids, tile_size)
    gradient = jnp.einsum(
        "tsk,tsn->skn", left_picked, right_picked, preferred_element_type=jnp.float32
    )
    return jnp.where(live_mask[:, None, None], gradient, jnp.zeros_like(gradient))


def gated_units(gate_sum, up_sum, hidden_grad):
    sigmoid_gate = jax.nn.sigmoid(gate_sum)
    active = gate_sum * sigmoid_gate
    hidden = (active * up_sum).astype(jnp.bfloat16)
    gate_act = (
        hidden_grad * up_sum * sigmoid_gate * (1.0 + gate_sum * (1.0 - sigmoid_gate))
    ).astype(jnp.bfloat16)
    up_act = (hidden_grad * active).astype(jnp.bfloat16)
    return (hidden, gate_act, up_act)


def dense_body(tokens, cotangent, gate_tiles, up_tiles, down_tiles, tile_index, tile_counts):
    tile_size = gate_tiles.shape[-1]
    row_blocks = tokens.shape[1] // tile_size
    col_blocks = FF // lax.axis_size("col") // tile_size
    slot_ids = jnp.arange(gate_tiles.shape[0])
    gate_live = slot_ids < tile_counts[0, 0, 0]
    up_live = slot_ids < tile_counts[1, 0, 0]
    down_live = slot_ids < tile_counts[2, 0, 0]
    gate_in, gate_out = (tile_index[0, :, 0], tile_index[0, :, 1])
    up_in, up_out = (tile_index[1, :, 0], tile_index[1, :, 1])
    down_in, down_out = (tile_index[2, :, 0], tile_index[2, :, 1])
    whole_tokens, whole_cotangent = (
        lax.all_gather(tokens, "col", axis=0, tiled=True),
        lax.all_gather(cotangent, "col", axis=0, tiled=True),
    )
    gate_part = sparse_apply(whole_tokens, gate_tiles, gate_in, gate_out, gate_live, col_blocks)
    up_part = sparse_apply(whole_tokens, up_tiles, up_in, up_out, up_live, col_blocks)
    grad_part = sparse_apply_back(
        whole_cotangent, down_tiles, down_out, down_in, down_live, col_blocks
    )
    gate_sum, up_sum, hidden_grad = (
        lax.psum_scatter(gate_part, "row", scatter_dimension=0, tiled=True),
        lax.psum_scatter(up_part, "row", scatter_dimension=0, tiled=True),
        lax.psum_scatter(grad_part, "row", scatter_dimension=0, tiled=True),
    )
    hidden, gate_act, up_act = gated_units(gate_sum, up_sum, hidden_grad)
    hidden_all, gate_all, up_all = (
        lax.all_gather(hidden, "row", axis=0, tiled=True),
        lax.all_gather(gate_act, "row", axis=0, tiled=True),
        lax.all_gather(up_act, "row", axis=0, tiled=True),
    )
    output_part = sparse_apply(hidden_all, down_tiles, down_in, down_out, down_live, row_blocks)
    input_part = sparse_apply_back(gate_all, gate_tiles, gate_out, gate_in, gate_live, row_blocks)
    input_part = input_part + sparse_apply_back(
        up_all, up_tiles, up_out, up_in, up_live, row_blocks
    )
    output_sum, input_sum = (
        lax.psum_scatter(output_part, "col", scatter_dimension=0, tiled=True),
        lax.psum_scatter(input_part, "col", scatter_dimension=0, tiled=True),
    )
    output = output_sum.astype(jnp.bfloat16)
    input_grad = input_sum.astype(jnp.bfloat16)
    gate_grad = tile_grads(whole_tokens, gate_all, gate_in, gate_out, gate_live, tile_size)
    up_grad = tile_grads(whole_tokens, up_all, up_in, up_out, up_live, tile_size)
    down_grad = tile_grads(hidden_all, whole_cotangent, down_in, down_out, down_live, tile_size)
    return (output, input_grad, gate_grad, up_grad, down_grad)


MESH = pl.DeviceIdType.MESH
F32 = jnp.float32
BF16 = jnp.bfloat16
NT = (((1,), (1,)), ((), ()))
NN = (((1,), (0,)), ((), ()))
TN = (((0,), (0,)), ((), ()))


def dot(a, b, dims):
    return lax.dot_general(a, b, dims, preferred_element_type=F32)


def pair_at(matrix, slot, side, slots):
    return (matrix * slots + slot) * 2 + side


def exchange_kernel(
    C, S, T, RB, CB, tile,
    meta, tok, cot, gate_t, up_t, down_t,
    got_out, meta_out, gate_g, up_g, down_g,
    meta_v, meta_s, blocks, pack, send_a, recv_a, X, P, Pb, recv_b, acts, Q, send_c, recv_c,
    m_send, m_recv, a_send, a_recv, b_send, b_recv, c_send, c_recv, local_sem,
):
    N = C * T
    mc, mr = lax.axis_index("col"), lax.axis_index("row")
    partner = 1 - mr
    tiles = (gate_t, up_t, down_t)
    grads = (gate_g, up_g, down_g)
    n_meta = 3 * S * 2

    barrier = pltpu.get_barrier_semaphore()

    def greet(k, _):
        pl.semaphore_signal(barrier, inc=1, device_id={"col": lax.rem(mc + k, C)}, device_id_type=MESH)
        return 0

    lax.fori_loop(1, C, greet, 0)
    pl.semaphore_signal(barrier, inc=1, device_id={"row": partner}, device_id_type=MESH)
    pl.semaphore_wait(barrier, C)

    def meta_copy(k, owner, target):
        return pltpu.make_async_remote_copy(
            src_ref=meta, dst_ref=meta_v.at[owner], send_sem=m_send.at[k], recv_sem=m_recv.at[k],
            device_id={"col": target}, device_id_type=MESH,
        )

    def meta_row(owner):
        return pltpu.make_async_remote_copy(
            src_ref=meta, dst_ref=meta_v.at[C + owner], send_sem=m_send.at[0], recv_sem=m_recv.at[0],
            device_id={"row": partner}, device_id_type=MESH,
        )

    def meta_start(k, _):
        meta_copy(k, mc, lax.rem(mc + k, C)).start()
        return 0

    lax.fori_loop(1, C, meta_start, 0)
    meta_row(mr).start()
    meta_v[mc] = meta[...]
    meta_v[C + mr] = meta[...]
    for b in range(RB):
        blocks[b, 0:T, :] = tok[:, b * tile:(b + 1) * tile].astype(F32)
        blocks[RB + b, 0:T, :] = cot[:, b * tile:(b + 1) * tile].astype(F32)
    pack[...] = jnp.zeros_like(pack)

    def meta_wait(k, _):
        meta_copy(k, lax.rem(mc - k + C, C), lax.rem(mc + k, C)).wait()
        return 0

    lax.fori_loop(1, C, meta_wait, 0)
    meta_row(partner).wait()
    to_smem = pltpu.make_async_copy(meta_v, meta_s, local_sem)
    to_smem.start()
    to_smem.wait()

    def a_copy(k, owner, target):
        return pltpu.make_async_remote_copy(
            src_ref=send_a.at[k], dst_ref=recv_a.at[owner], send_sem=a_send.at[k], recv_sem=a_recv.at[k],
            device_id={"col": target}, device_id_type=MESH,
        )

    def pick_for(dest):
        for s in range(3 * S):
            m = s // S
            side, base = (1, RB) if m == 2 else (0, 0)
            b = meta_s[dest, 0, pair_at(m, s % S, side, S)] + base
            pack[s * T:(s + 1) * T, :] = blocks[b, 0:T, :]

    def a_start(k, _):
        dest = lax.rem(mc + k, C)
        pick_for(dest)
        send_a[k] = pack[...].astype(BF16)
        a_copy(k, mc, dest).start()
        return 0

    lax.fori_loop(1, C, a_start, 0)
    pick_for(mc)
    for s in range(3 * S):
        X[s, 0:T, :] = pack[s * T:(s + 1) * T, :]

    def a_wait(k, _):
        src = lax.rem(mc - k + C, C)
        a_copy(k, src, lax.rem(mc + k, C)).wait()
        pack[...] = recv_a[src].astype(F32)
        for s in range(3 * S):
            X[s, pl.ds(k * T, T), :] = pack[s * T:(s + 1) * T, :]
        return 0

    lax.fori_loop(1, C, a_wait, 0)

    def live(m, s):
        return s < meta_s[mc, 0, n_meta + m]

    def b_copy(m):
        return pltpu.make_async_remote_copy(
            src_ref=Pb.at[m], dst_ref=recv_b.at[m], send_sem=b_send.at[m], recv_sem=b_recv.at[m],
            device_id={"row": partner}, device_id_type=MESH,
        )

    for m in range(3):
        def product(s, _, m=m):
            part = dot(X[m * S + s].astype(BF16), tiles[m][s], NT if m == 2 else NN)
            part = jnp.where(live(m, s), part, 0.0)
            P[m * S + s] = part
            Pb[m, s] = part.astype(BF16)
            return 0

        lax.fori_loop(0, S, product, 0)
        b_copy(m).start()
    for m in range(3):
        b_copy(m).wait()

    step = N // 2 if N % 32 == 0 else N

    def activate(j, _):
        for half in range(N // step):
            rows = slice(half * step, (half + 1) * step)
            sums = []
            for m in range(3):
                side = 0 if m == 2 else 1
                total = jnp.zeros((step, tile), F32)
                for s in range(S):
                    at = pair_at(m, s, side, S)
                    total = total + jnp.where(meta_s[mc, 0, at] == j, P[m * S + s, rows, :], 0.0)
                    total = total + jnp.where(
                        meta_s[C + partner, 0, at] == j, recv_b[m, s, rows, :].astype(F32), 0.0
                    )
                sums.append(total)
            g, u, hg = sums
            sg = jax.nn.sigmoid(g)
            active = g * sg
            acts[0, j, rows, :] = (hg * u * sg * (1.0 + g * (1.0 - sg))).astype(BF16)
            acts[1, j, rows, :] = (hg * active).astype(BF16)
            acts[2, j, rows, :] = (active * u).astype(BF16)
        return 0

    lax.fori_loop(0, CB, activate, 0)

    for m in range(3):
        def back(s, _, m=m):
            j = meta_s[mc, 0, pair_at(m, s, 0 if m == 2 else 1, S)]
            part = dot(acts[m, j], tiles[m][s], NN if m == 2 else NT)
            Q[m * S + s] = jnp.where(live(m, s), part, 0.0)
            return 0

        lax.fori_loop(0, S, back, 0)

    def c_copy(k, owner, target):
        return pltpu.make_async_remote_copy(
            src_ref=send_c.at[k], dst_ref=recv_c.at[owner], send_sem=c_send.at[k], recv_sem=c_recv.at[k],
            device_id={"col": target}, device_id_type=MESH,
        )

    def c_start(k, _):
        for s in range(3 * S):
            pack[s * T:(s + 1) * T, :] = Q[s, pl.ds(k * T, T), :]
        send_c[k] = pack[...].astype(BF16)
        c_copy(k, mc, lax.rem(mc - k + C, C)).start()
        return 0

    lax.fori_loop(1, C, c_start, 0)
    for s in range(3 * S):
        pack[s * T:(s + 1) * T, :] = Q[s, 0:T, :]
    got_out[mc] = pack[...].astype(BF16)
    meta_out[...] = meta_v[...]

    for m in range(3):
        def tile_grad(s, _, m=m):
            j = meta_s[mc, 0, pair_at(m, s, 0 if m == 2 else 1, S)]
            x = X[m * S + s].astype(BF16)
            part = dot(acts[m, j], x, TN) if m == 2 else dot(x, acts[m, j], TN)
            grads[m][s] = jnp.where(live(m, s), part, 0.0)
            return 0

        lax.fori_loop(0, S, tile_grad, 0)

    def c_wait(k, _):
        src = lax.rem(mc + k, C)
        c_copy(k, src, lax.rem(mc - k + C, C)).wait()
        got_out[src] = recv_c[src]
        return 0

    lax.fori_loop(1, C, c_wait, 0)


def add_kernel(C, S, T, RB, tile, meta, got, out, ingrad, total, pack):
    total[...] = jnp.zeros_like(total)

    def add(c, _):
        pack[...] = got[c].astype(F32)
        for s in range(3 * S):
            m = s // S
            side, base = (1, RB) if m == 2 else (0, 0)
            b = meta[c, 0, pair_at(m, s % S, side, S)] + base
            total[b, 0:T, :] += pack[s * T:(s + 1) * T, :]
        return 0

    lax.fori_loop(0, C, add, 0)
    for b in range(RB):
        ingrad[:, b * tile:(b + 1) * tile] = total[b, 0:T, :].astype(BF16)
        out[:, b * tile:(b + 1) * tile] = total[RB + b, 0:T, :].astype(BF16)


def sparse_body(tokens, cotangent, gate_tiles, up_tiles, down_tiles, tile_index, tile_counts):
    C, R = lax.axis_size("col"), lax.axis_size("row")
    T, width = tokens.shape
    S, tile = gate_tiles.shape[0], gate_tiles.shape[-1]
    RB, CB = width // tile, FF // C // tile
    N = C * T
    rows = -(-3 * S * T // 16) * 16
    pad_t = -(-T // 8) * 8
    meta = jnp.concatenate([tile_index.reshape(-1), tile_counts.reshape(-1)])
    meta = jnp.pad(meta, (0, 1024 - meta.shape[0])).reshape(8, 128)
    V, M = pltpu.VMEM, pltpu.SemaphoreType.DMA
    vspec = pl.BlockSpec(memory_space=pltpu.VMEM)
    sd = jax.ShapeDtypeStruct
    got, metas, gate_grad, up_grad, down_grad = pl.pallas_call(
        functools.partial(exchange_kernel, C, S, T, RB, CB, tile),
        out_shape=[sd((C, rows, tile), BF16), sd((C + R, 8, 128), jnp.int32)]
        + [sd((S, tile, tile), F32)] * 3,
        in_specs=[vspec] * 6,
        out_specs=[vspec] * 5,
        scratch_shapes=[
            V((C + R, 8, 128), jnp.int32),
            pltpu.SMEM((C + R, 8, 128), jnp.int32),
            V((2 * RB, pad_t, tile), F32),
            V((rows, tile), F32),
            V((C, rows, tile), BF16),
            V((C, rows, tile), BF16),
            V((3 * S, N, tile), F32),
            V((3 * S, N, tile), F32),
            V((3, S, N, tile), BF16),
            V((3, S, N, tile), BF16),
            V((3, CB, N, tile), BF16),
            V((3 * S, N, tile), F32),
            V((C, rows, tile), BF16),
            V((C, rows, tile), BF16),
            M((C,)), M((C,)), M((C,)), M((C,)), M((3,)), M((3,)), M((C,)), M((C,)), M,
        ],
        compiler_params=pltpu.CompilerParams(
            collective_id=0, has_side_effects=True, vmem_limit_bytes=40 * 1024 * 1024
        ),
        name="exchange",
    )(meta, tokens, cotangent, gate_tiles, up_tiles, down_tiles)
    output, input_grad = pl.pallas_call(
        functools.partial(add_kernel, C, S, T, RB, tile),
        out_shape=[sd((T, width), BF16)] * 2,
        in_specs=[pl.BlockSpec(memory_space=pltpu.SMEM), vspec],
        out_specs=[vspec] * 2,
        scratch_shapes=[V((2 * RB, pad_t, tile), F32), V((rows, tile), F32)],
        compiler_params=pltpu.CompilerParams(vmem_limit_bytes=16 * 1024 * 1024),
        name="add_slots",
    )(metas, got)
    return (output, input_grad, gate_grad, up_grad, down_grad)


def solution(mesh):
    body = sparse_body if mesh.shape["row"] == 2 else dense_body
    return jax.shard_map(
        body,
        mesh=mesh,
        in_specs=(
            P("col", "row"),
            P("col", "row"),
            P("row", "col", None),
            P("row", "col", None),
            P("row", "col", None),
            P(None, "row", "col"),
            P(None, "row", "col"),
        ),
        out_specs=(
            P("col", "row"),
            P("col", "row"),
            P("row", "col", None),
            P("row", "col", None),
            P("row", "col", None),
        ),
        check_vma=False,
    )
```

```python
import functools

import jax
import jax.numpy as jnp
from jax import lax
from jax.experimental import pallas as pl
from jax.experimental.pallas import tpu as pltpu
from jax.sharding import PartitionSpec as P

FF = 16384


def pick_blocks(data_rows, block_ids, tile_size):
    token_count = data_rows.shape[0]
    block_count = data_rows.shape[1] // tile_size
    split_rows = data_rows.reshape(token_count, block_count, tile_size)
    select = (block_ids[:, None] == jnp.arange(block_count)[None, :]).astype(jnp.bfloat16)
    picked = jnp.einsum("tbk,sb->tsk", split_rows, select, preferred_element_type=jnp.float32)
    return picked.astype(jnp.bfloat16)


def place_blocks(products, block_ids, live_mask, block_count):
    select = ((block_ids[:, None] == jnp.arange(block_count)[None, :]) & live_mask[:, None]).astype(
        jnp.float32
    )
    placed = jnp.einsum("tsn,sc->tcn", products, select, precision=lax.Precision.HIGHEST)
    return placed.reshape(products.shape[0], block_count * products.shape[2])


def sparse_apply(data_rows, tiles, in_ids, out_ids, live_mask, out_count):
    picked = pick_blocks(data_rows, in_ids, tiles.shape[-1])
    products = jnp.einsum("tsk,skn->tsn", picked, tiles, preferred_element_type=jnp.float32)
    return place_blocks(products, out_ids, live_mask, out_count)


def sparse_apply_back(data_rows, tiles, in_ids, out_ids, live_mask, out_count):
    picked = pick_blocks(data_rows, in_ids, tiles.shape[-1])
    products = jnp.einsum("tsn,skn->tsk", picked, tiles, preferred_element_type=jnp.float32)
    return place_blocks(products, out_ids, live_mask, out_count)


def tile_grads(left_rows, right_rows, left_ids, right_ids, live_mask, tile_size):
    left_picked = pick_blocks(left_rows, left_ids, tile_size)
    right_picked = pick_blocks(right_rows, right_ids, tile_size)
    gradient = jnp.einsum(
        "tsk,tsn->skn", left_picked, right_picked, preferred_element_type=jnp.float32
    )
    return jnp.where(live_mask[:, None, None], gradient, jnp.zeros_like(gradient))


def gated_units(gate_sum, up_sum, hidden_grad):
    sigmoid_gate = jax.nn.sigmoid(gate_sum)
    active = gate_sum * sigmoid_gate
    hidden = (active * up_sum).astype(jnp.bfloat16)
    gate_act = (
        hidden_grad * up_sum * sigmoid_gate * (1.0 + gate_sum * (1.0 - sigmoid_gate))
    ).astype(jnp.bfloat16)
    up_act = (hidden_grad * active).astype(jnp.bfloat16)
    return (hidden, gate_act, up_act)


def dense_body(tokens, cotangent, gate_tiles, up_tiles, down_tiles, tile_index, tile_counts):
    tile_size = gate_tiles.shape[-1]
    row_blocks = tokens.shape[1] // tile_size
    col_blocks = FF // lax.axis_size("col") // tile_size
    slot_ids = jnp.arange(gate_tiles.shape[0])
    gate_live = slot_ids < tile_counts[0, 0, 0]
    up_live = slot_ids < tile_counts[1, 0, 0]
    down_live = slot_ids < tile_counts[2, 0, 0]
    gate_in, gate_out = (tile_index[0, :, 0], tile_index[0, :, 1])
    up_in, up_out = (tile_index[1, :, 0], tile_index[1, :, 1])
    down_in, down_out = (tile_index[2, :, 0], tile_index[2, :, 1])
    whole_tokens, whole_cotangent = (
        lax.all_gather(tokens, "col", axis=0, tiled=True),
        lax.all_gather(cotangent, "col", axis=0, tiled=True),
    )
    gate_part = sparse_apply(whole_tokens, gate_tiles, gate_in, gate_out, gate_live, col_blocks)
    up_part = sparse_apply(whole_tokens, up_tiles, up_in, up_out, up_live, col_blocks)
    grad_part = sparse_apply_back(
        whole_cotangent, down_tiles, down_out, down_in, down_live, col_blocks
    )
    gate_sum, up_sum, hidden_grad = (
        lax.psum_scatter(gate_part, "row", scatter_dimension=0, tiled=True),
        lax.psum_scatter(up_part, "row", scatter_dimension=0, tiled=True),
        lax.psum_scatter(grad_part, "row", scatter_dimension=0, tiled=True),
    )
    hidden, gate_act, up_act = gated_units(gate_sum, up_sum, hidden_grad)
    hidden_all, gate_all, up_all = (
        lax.all_gather(hidden, "row", axis=0, tiled=True),
        lax.all_gather(gate_act, "row", axis=0, tiled=True),
        lax.all_gather(up_act, "row", axis=0, tiled=True),
    )
    output_part = sparse_apply(hidden_all, down_tiles, down_in, down_out, down_live, row_blocks)
    input_part = sparse_apply_back(gate_all, gate_tiles, gate_out, gate_in, gate_live, row_blocks)
    input_part = input_part + sparse_apply_back(
        up_all, up_tiles, up_out, up_in, up_live, row_blocks
    )
    output_sum, input_sum = (
        lax.psum_scatter(output_part, "col", scatter_dimension=0, tiled=True),
        lax.psum_scatter(input_part, "col", scatter_dimension=0, tiled=True),
    )
    output = output_sum.astype(jnp.bfloat16)
    input_grad = input_sum.astype(jnp.bfloat16)
    gate_grad = tile_grads(whole_tokens, gate_all, gate_in, gate_out, gate_live, tile_size)
    up_grad = tile_grads(whole_tokens, up_all, up_in, up_out, up_live, tile_size)
    down_grad = tile_grads(hidden_all, whole_cotangent, down_in, down_out, down_live, tile_size)
    return (output, input_grad, gate_grad, up_grad, down_grad)


MESH = pl.DeviceIdType.MESH
F32 = jnp.float32
BF16 = jnp.bfloat16
NT = (((1,), (1,)), ((), ()))
NN = (((1,), (0,)), ((), ()))
TN = (((0,), (0,)), ((), ()))


def dot(a, b, dims):
    return lax.dot_general(a, b, dims, preferred_element_type=F32)


def exchange_kernel(
    C, S, T, RB, CB, tile, G,
    index, counts, tok, cot, gate_t, up_t, down_t,
    got_out, meta_out, gate_g, up_g, down_g,
    index_v, counts_v, meta, tiles_v, grads_v,
    meta_v, meta_s, blocks, pack, send_a, recv_a, X, P, Pb, recv_b, acts, Q, send_c, recv_c,
    m_send, m_recv, a_send, a_recv, b_send, b_recv, c_send, c_recv, in_sem, out_sem, local_sem,
):
    N = C * T
    H, peers = N // G, C // G
    mc, mr = lax.axis_index("col"), lax.axis_index("row")
    partner = 1 - mr
    index_copy = pltpu.make_async_copy(index, index_v, in_sem.at[3])
    counts_copy = pltpu.make_async_copy(counts, counts_v, in_sem.at[4])
    tile_copies = [
        pltpu.make_async_copy(ref, tiles_v.at[m], in_sem.at[m])
        for m, ref in enumerate((gate_t, up_t, down_t))
    ]
    grad_copies = [
        pltpu.make_async_copy(grads_v.at[m], ref, out_sem.at[m])
        for m, ref in enumerate((gate_g, up_g, down_g))
    ]
    index_copy.start()
    counts_copy.start()
    for copy in tile_copies:
        copy.start()

    barrier = pltpu.get_barrier_semaphore()

    def greet(k, _):
        pl.semaphore_signal(barrier, inc=1, device_id={"col": lax.rem(mc + k, C)}, device_id_type=MESH)
        return 0

    lax.fori_loop(1, C, greet, 0)
    pl.semaphore_signal(barrier, inc=1, device_id={"row": partner}, device_id_type=MESH)
    index_copy.wait()
    counts_copy.wait()
    meta[...] = jnp.zeros_like(meta)
    for m in range(3):
        meta[0:S, 2 * m:2 * m + 2] = index_v[m]
        meta[S:S + 1, m:m + 1] = counts_v[m]
    pl.semaphore_wait(barrier, C)

    def meta_copy(k, owner, target):
        return pltpu.make_async_remote_copy(
            src_ref=meta, dst_ref=meta_v.at[owner], send_sem=m_send.at[k], recv_sem=m_recv.at[k],
            device_id={"col": target}, device_id_type=MESH,
        )

    def meta_row(owner):
        return pltpu.make_async_remote_copy(
            src_ref=meta, dst_ref=meta_v.at[C + owner], send_sem=m_send.at[0], recv_sem=m_recv.at[0],
            device_id={"row": partner}, device_id_type=MESH,
        )

    def meta_start(k, _):
        meta_copy(k, mc, lax.rem(mc + k, C)).start()
        return 0

    lax.fori_loop(1, C, meta_start, 0)
    meta_row(mr).start()
    meta_v[mc] = meta[...]
    meta_v[C + mr] = meta[...]
    for b in range(RB):
        blocks[b, 0:T, :] = tok[:, b * tile:(b + 1) * tile].astype(F32)
        blocks[RB + b, 0:T, :] = cot[:, b * tile:(b + 1) * tile].astype(F32)
    pack[...] = jnp.zeros_like(pack)

    def meta_wait(k, _):
        meta_copy(k, lax.rem(mc - k + C, C), lax.rem(mc + k, C)).wait()
        return 0

    lax.fori_loop(1, C, meta_wait, 0)
    meta_row(partner).wait()
    to_smem = pltpu.make_async_copy(meta_v, meta_s, local_sem)
    to_smem.start()
    to_smem.wait()

    def a_copy(k, owner, target):
        return pltpu.make_async_remote_copy(
            src_ref=send_a.at[k], dst_ref=recv_a.at[owner], send_sem=a_send.at[k], recv_sem=a_recv.at[k],
            device_id={"col": target}, device_id_type=MESH,
        )

    def pick_for(dest):
        for s in range(3 * S):
            m = s // S
            side, base = (1, RB) if m == 2 else (0, 0)
            b = meta_s[dest, s % S, 2 * m + side] + base
            pack[s * T:(s + 1) * T, :] = blocks[b, 0:T, :]

    def a_start(k, _):
        dest = lax.rem(mc + k, C)
        pick_for(dest)
        send_a[k] = pack[...].astype(BF16)
        a_copy(k, mc, dest).start()
        return 0

    lax.fori_loop(1, C, a_start, 0)
    pick_for(mc)
    for s in range(3 * S):
        X[s, 0:T, :] = pack[s * T:(s + 1) * T, :]

    def a_wait(k, _):
        src = lax.rem(mc - k + C, C)
        a_copy(k, src, lax.rem(mc + k, C)).wait()
        pack[...] = recv_a[src].astype(F32)
        for s in range(3 * S):
            X[s, pl.ds(k * T, T), :] = pack[s * T:(s + 1) * T, :]
        return 0

    def live(m, s):
        return s < meta_s[mc, S, m]

    def b_copy(g, m):
        return pltpu.make_async_remote_copy(
            src_ref=Pb.at[g, m], dst_ref=recv_b.at[g, m],
            send_sem=b_send.at[g, m], recv_sem=b_recv.at[g, m],
            device_id={"row": partner}, device_id_type=MESH,
        )

    for g in range(G):
        rows = slice(g * H, (g + 1) * H)
        lax.fori_loop(max(1, g * peers), (g + 1) * peers, a_wait, 0)
        if g == 0:
            for copy in tile_copies:
                copy.wait()
        for m in range(3):
            def product(s, _, m=m, g=g, rows=rows):
                part = dot(X[m * S + s, rows, :].astype(BF16), tiles_v[m, s], NT if m == 2 else NN)
                part = jnp.where(live(m, s), part, 0.0)
                P[m * S + s, rows, :] = part
                Pb[g, m, s] = part.astype(BF16)
                return 0

            lax.fori_loop(0, S, product, 0)
            b_copy(g, m).start()

    def c_copy(k, owner, target):
        return pltpu.make_async_remote_copy(
            src_ref=send_c.at[k], dst_ref=recv_c.at[owner], send_sem=c_send.at[k], recv_sem=c_recv.at[k],
            device_id={"col": target}, device_id_type=MESH,
        )

    def c_start(k, _):
        for s in range(3 * S):
            pack[s * T:(s + 1) * T, :] = Q[s, pl.ds(k * T, T), :]
        send_c[k] = pack[...].astype(BF16)
        c_copy(k, mc, lax.rem(mc - k + C, C)).start()
        return 0

    for g in range(G):
        rows = slice(g * H, (g + 1) * H)
        for m in range(3):
            b_copy(g, m).wait()

        def activate(j, _, g=g, rows=rows):
            sums = []
            for m in range(3):
                side = 0 if m == 2 else 1
                total = jnp.zeros((H, tile), F32)
                for s in range(S):
                    mine = meta_s[mc, s, 2 * m + side] == j
                    theirs = meta_s[C + partner, s, 2 * m + side] == j
                    total = total + jnp.where(mine, P[m * S + s, rows, :], 0.0)
                    total = total + jnp.where(theirs, recv_b[g, m, s].astype(F32), 0.0)
                sums.append(total)
            gate, up, hg = sums
            sg = jax.nn.sigmoid(gate)
            active = gate * sg
            acts[0, j, rows, :] = (hg * up * sg * (1.0 + gate * (1.0 - sg))).astype(BF16)
            acts[1, j, rows, :] = (hg * active).astype(BF16)
            acts[2, j, rows, :] = (active * up).astype(BF16)
            return 0

        lax.fori_loop(0, CB, activate, 0)

        for m in range(3):
            def back(s, _, m=m, rows=rows):
                j = meta_s[mc, s, 2 * m + (0 if m == 2 else 1)]
                part = dot(acts[m, j, rows, :], tiles_v[m, s], NN if m == 2 else NT)
                Q[m * S + s, rows, :] = jnp.where(live(m, s), part, 0.0)
                return 0

            lax.fori_loop(0, S, back, 0)
        lax.fori_loop(max(1, g * peers), (g + 1) * peers, c_start, 0)

    for s in range(3 * S):
        pack[s * T:(s + 1) * T, :] = Q[s, 0:T, :]
    got_out[mc] = pack[...].astype(BF16)
    meta_out[...] = meta_v[...]

    for m in range(3):
        def tile_grad(s, _, m=m):
            j = meta_s[mc, s, 2 * m + (0 if m == 2 else 1)]
            x = X[m * S + s].astype(BF16)
            part = dot(acts[m, j], x, TN) if m == 2 else dot(x, acts[m, j], TN)
            grads_v[m, s] = jnp.where(live(m, s), part, 0.0)
            return 0

        lax.fori_loop(0, S, tile_grad, 0)
        grad_copies[m].start()

    def c_wait(k, _):
        src = lax.rem(mc + k, C)
        c_copy(k, src, lax.rem(mc - k + C, C)).wait()
        got_out[src] = recv_c[src]
        return 0

    lax.fori_loop(1, C, c_wait, 0)
    for copy in grad_copies:
        copy.wait()


def add_kernel(
    C, S, T, RB, tile, meta, got, gate_in, up_in, down_in,
    out, ingrad, gate_g, up_g, down_g, total, pack, sem,
):
    copies = [
        pltpu.make_async_copy(src, dst, sem.at[m])
        for m, (src, dst) in enumerate(((gate_in, gate_g), (up_in, up_g), (down_in, down_g)))
    ]
    for copy in copies:
        copy.start()
    total[...] = jnp.zeros_like(total)

    def add(c, _):
        pack[...] = got[c].astype(F32)
        for s in range(3 * S):
            m = s // S
            side, base = (1, RB) if m == 2 else (0, 0)
            b = meta[c, s % S, 2 * m + side] + base
            total[b, 0:T, :] += pack[s * T:(s + 1) * T, :]
        return 0

    lax.fori_loop(0, C, add, 0)
    for b in range(RB):
        ingrad[:, b * tile:(b + 1) * tile] = total[b, 0:T, :].astype(BF16)
        out[:, b * tile:(b + 1) * tile] = total[RB + b, 0:T, :].astype(BF16)
    for copy in copies:
        copy.wait()


def sparse_body(tokens, cotangent, gate_tiles, up_tiles, down_tiles, tile_index, tile_counts):
    C, R = lax.axis_size("col"), lax.axis_size("row")
    T, width = tokens.shape
    S, tile = gate_tiles.shape[0], gate_tiles.shape[-1]
    RB, CB = width // tile, FF // C // tile
    N = C * T
    rows = -(-3 * S * T // 16) * 16
    pad_t = -(-T // 8) * 8
    G = 2 if C % 2 == 0 and (N // 2) % 16 == 0 else 1
    H = N // G
    meta_rows = -(-(S + 1) // 8) * 8
    V, M = pltpu.VMEM, pltpu.SemaphoreType.DMA
    vspec = pl.BlockSpec(memory_space=pltpu.VMEM)
    hbm = pl.BlockSpec(memory_space=pl.ANY)
    sd = jax.ShapeDtypeStruct
    got, metas, gate_grad, up_grad, down_grad = pl.pallas_call(
        functools.partial(exchange_kernel, C, S, T, RB, CB, tile, G),
        out_shape=[sd((C, rows, tile), BF16), sd((C + R, meta_rows, 128), jnp.int32)]
        + [sd((S, tile, tile), F32)] * 3,
        in_specs=[hbm] * 2 + [vspec] * 2 + [hbm] * 3,
        out_specs=[vspec] * 2 + [hbm] * 3,
        scratch_shapes=[
            V(tile_index.shape, jnp.int32),
            V(tile_counts.shape, jnp.int32),
            V((meta_rows, 128), jnp.int32),
            V((3, S, tile, tile), BF16),
            V((3, S, tile, tile), F32),
            V((C + R, meta_rows, 128), jnp.int32),
            pltpu.SMEM((C + R, meta_rows, 128), jnp.int32),
            V((2 * RB, pad_t, tile), F32),
            V((rows, tile), F32),
            V((C, rows, tile), BF16),
            V((C, rows, tile), BF16),
            V((3 * S, N, tile), F32),
            V((3 * S, N, tile), F32),
            V((G, 3, S, H, tile), BF16),
            V((G, 3, S, H, tile), BF16),
            V((3, CB, N, tile), BF16),
            V((3 * S, N, tile), F32),
            V((C, rows, tile), BF16),
            V((C, rows, tile), BF16),
            M((C,)), M((C,)), M((C,)), M((C,)), M((G, 3)), M((G, 3)), M((C,)), M((C,)),
            M((5,)), M((3,)), M,
        ],
        compiler_params=pltpu.CompilerParams(
            collective_id=0, has_side_effects=True, vmem_limit_bytes=40 * 1024 * 1024
        ),
        name="exchange",
    )(tile_index, tile_counts, tokens, cotangent, gate_tiles, up_tiles, down_tiles)
    return pl.pallas_call(
        functools.partial(add_kernel, C, S, T, RB, tile),
        out_shape=[sd((T, width), BF16)] * 2 + [sd((S, tile, tile), F32)] * 3,
        in_specs=[pl.BlockSpec(memory_space=pltpu.SMEM), vspec] + [hbm] * 3,
        out_specs=[vspec] * 2 + [hbm] * 3,
        scratch_shapes=[V((2 * RB, pad_t, tile), F32), V((rows, tile), F32), M((3,))],
        compiler_params=pltpu.CompilerParams(vmem_limit_bytes=16 * 1024 * 1024),
        name="add_slots",
    )(metas, got, gate_grad, up_grad, down_grad)


def solution(mesh):
    body = sparse_body if mesh.shape["row"] == 2 else dense_body
    return jax.shard_map(
        body,
        mesh=mesh,
        in_specs=(
            P("col", "row"),
            P("col", "row"),
            P("row", "col", None),
            P("row", "col", None),
            P("row", "col", None),
            P(None, "row", "col"),
            P(None, "row", "col"),
        ),
        out_specs=(
            P("col", "row"),
            P("col", "row"),
            P("row", "col", None),
            P("row", "col", None),
            P("row", "col", None),
        ),
        check_vma=False,
    )
```

```python
import functools

import jax
import jax.numpy as jnp
from jax import lax
from jax.experimental import pallas as pl
from jax.experimental.pallas import tpu as pltpu
from jax.sharding import PartitionSpec as P

FF = 16384


def pick_blocks(data_rows, block_ids, tile_size):
    token_count = data_rows.shape[0]
    block_count = data_rows.shape[1] // tile_size
    split_rows = data_rows.reshape(token_count, block_count, tile_size)
    select = (block_ids[:, None] == jnp.arange(block_count)[None, :]).astype(jnp.bfloat16)
    picked = jnp.einsum("tbk,sb->tsk", split_rows, select, preferred_element_type=jnp.float32)
    return picked.astype(jnp.bfloat16)


def place_blocks(products, block_ids, live_mask, block_count):
    select = ((block_ids[:, None] == jnp.arange(block_count)[None, :]) & live_mask[:, None]).astype(
        jnp.float32
    )
    placed = jnp.einsum("tsn,sc->tcn", products, select, precision=lax.Precision.HIGHEST)
    return placed.reshape(products.shape[0], block_count * products.shape[2])


def sparse_apply(data_rows, tiles, in_ids, out_ids, live_mask, out_count):
    picked = pick_blocks(data_rows, in_ids, tiles.shape[-1])
    products = jnp.einsum("tsk,skn->tsn", picked, tiles, preferred_element_type=jnp.float32)
    return place_blocks(products, out_ids, live_mask, out_count)


def sparse_apply_back(data_rows, tiles, in_ids, out_ids, live_mask, out_count):
    picked = pick_blocks(data_rows, in_ids, tiles.shape[-1])
    products = jnp.einsum("tsn,skn->tsk", picked, tiles, preferred_element_type=jnp.float32)
    return place_blocks(products, out_ids, live_mask, out_count)


def tile_grads(left_rows, right_rows, left_ids, right_ids, live_mask, tile_size):
    left_picked = pick_blocks(left_rows, left_ids, tile_size)
    right_picked = pick_blocks(right_rows, right_ids, tile_size)
    gradient = jnp.einsum(
        "tsk,tsn->skn", left_picked, right_picked, preferred_element_type=jnp.float32
    )
    return jnp.where(live_mask[:, None, None], gradient, jnp.zeros_like(gradient))


def gated_units(gate_sum, up_sum, hidden_grad):
    sigmoid_gate = jax.nn.sigmoid(gate_sum)
    active = gate_sum * sigmoid_gate
    hidden = (active * up_sum).astype(jnp.bfloat16)
    gate_act = (
        hidden_grad * up_sum * sigmoid_gate * (1.0 + gate_sum * (1.0 - sigmoid_gate))
    ).astype(jnp.bfloat16)
    up_act = (hidden_grad * active).astype(jnp.bfloat16)
    return (hidden, gate_act, up_act)


def dense_body(tokens, cotangent, gate_tiles, up_tiles, down_tiles, tile_index, tile_counts):
    tile_size = gate_tiles.shape[-1]
    row_blocks = tokens.shape[1] // tile_size
    col_blocks = FF // lax.axis_size("col") // tile_size
    slot_ids = jnp.arange(gate_tiles.shape[0])
    gate_live = slot_ids < tile_counts[0, 0, 0]
    up_live = slot_ids < tile_counts[1, 0, 0]
    down_live = slot_ids < tile_counts[2, 0, 0]
    gate_in, gate_out = (tile_index[0, :, 0], tile_index[0, :, 1])
    up_in, up_out = (tile_index[1, :, 0], tile_index[1, :, 1])
    down_in, down_out = (tile_index[2, :, 0], tile_index[2, :, 1])
    whole_tokens, whole_cotangent = (
        lax.all_gather(tokens, "col", axis=0, tiled=True),
        lax.all_gather(cotangent, "col", axis=0, tiled=True),
    )
    gate_part = sparse_apply(whole_tokens, gate_tiles, gate_in, gate_out, gate_live, col_blocks)
    up_part = sparse_apply(whole_tokens, up_tiles, up_in, up_out, up_live, col_blocks)
    grad_part = sparse_apply_back(
        whole_cotangent, down_tiles, down_out, down_in, down_live, col_blocks
    )
    gate_sum, up_sum, hidden_grad = (
        lax.psum_scatter(gate_part, "row", scatter_dimension=0, tiled=True),
        lax.psum_scatter(up_part, "row", scatter_dimension=0, tiled=True),
        lax.psum_scatter(grad_part, "row", scatter_dimension=0, tiled=True),
    )
    hidden, gate_act, up_act = gated_units(gate_sum, up_sum, hidden_grad)
    hidden_all, gate_all, up_all = (
        lax.all_gather(hidden, "row", axis=0, tiled=True),
        lax.all_gather(gate_act, "row", axis=0, tiled=True),
        lax.all_gather(up_act, "row", axis=0, tiled=True),
    )
    output_part = sparse_apply(hidden_all, down_tiles, down_in, down_out, down_live, row_blocks)
    input_part = sparse_apply_back(gate_all, gate_tiles, gate_out, gate_in, gate_live, row_blocks)
    input_part = input_part + sparse_apply_back(
        up_all, up_tiles, up_out, up_in, up_live, row_blocks
    )
    output_sum, input_sum = (
        lax.psum_scatter(output_part, "col", scatter_dimension=0, tiled=True),
        lax.psum_scatter(input_part, "col", scatter_dimension=0, tiled=True),
    )
    output = output_sum.astype(jnp.bfloat16)
    input_grad = input_sum.astype(jnp.bfloat16)
    gate_grad = tile_grads(whole_tokens, gate_all, gate_in, gate_out, gate_live, tile_size)
    up_grad = tile_grads(whole_tokens, up_all, up_in, up_out, up_live, tile_size)
    down_grad = tile_grads(hidden_all, whole_cotangent, down_in, down_out, down_live, tile_size)
    return (output, input_grad, gate_grad, up_grad, down_grad)


MESH = pl.DeviceIdType.MESH
F32 = jnp.float32
BF16 = jnp.bfloat16
NT = (((1,), (1,)), ((), ()))
NN = (((1,), (0,)), ((), ()))
TN = (((0,), (0,)), ((), ()))


def dot(a, b, dims):
    return lax.dot_general(a, b, dims, preferred_element_type=F32)


def exchange_kernel(
    C, S, T, RB, CB, tile, G,
    index, counts, tok, cot, gate_t, up_t, down_t,
    got_out, meta_out, gate_g, up_g, down_g,
    index_v, counts_v, meta, tiles_v, grads_v,
    meta_v, meta_s, blocks, pack, send_a, recv_a, X, P, Pb, recv_b, sums, acts, Q, send_c,
    m_send, m_recv, a_send, a_recv, b_send, b_recv, c_send, c_recv, in_sem, out_sem, local_sem,
):
    N = C * T
    H, peers = N // G, C // G
    mc, mr = lax.axis_index("col"), lax.axis_index("row")
    partner = 1 - mr
    index_copy = pltpu.make_async_copy(index, index_v, in_sem.at[3])
    counts_copy = pltpu.make_async_copy(counts, counts_v, in_sem.at[4])
    tile_copies = [
        pltpu.make_async_copy(ref, tiles_v.at[m], in_sem.at[m])
        for m, ref in enumerate((gate_t, up_t, down_t))
    ]
    grad_copies = [
        pltpu.make_async_copy(grads_v.at[m], ref, out_sem.at[m])
        for m, ref in enumerate((gate_g, up_g, down_g))
    ]
    index_copy.start()
    counts_copy.start()
    for copy in tile_copies:
        copy.start()

    barrier = pltpu.get_barrier_semaphore()

    def greet(k, _):
        pl.semaphore_signal(barrier, inc=1, device_id={"col": lax.rem(mc + k, C)}, device_id_type=MESH)
        return 0

    lax.fori_loop(1, C, greet, 0)
    pl.semaphore_signal(barrier, inc=1, device_id={"row": partner}, device_id_type=MESH)
    index_copy.wait()
    counts_copy.wait()
    meta[...] = jnp.zeros_like(meta)
    for m in range(3):
        meta[2 * m:2 * m + 2, 0:S] = index_v[m]
    meta[6:7, 0:3] = counts_v[0]
    pl.semaphore_wait(barrier, C)

    def meta_copy(k, owner, target):
        return pltpu.make_async_remote_copy(
            src_ref=meta, dst_ref=meta_v.at[owner], send_sem=m_send.at[k], recv_sem=m_recv.at[k],
            device_id={"col": target}, device_id_type=MESH,
        )

    def meta_row(owner):
        return pltpu.make_async_remote_copy(
            src_ref=meta, dst_ref=meta_v.at[C + owner], send_sem=m_send.at[0], recv_sem=m_recv.at[0],
            device_id={"row": partner}, device_id_type=MESH,
        )

    def meta_start(k, _):
        meta_copy(k, mc, lax.rem(mc + k, C)).start()
        return 0

    lax.fori_loop(1, C, meta_start, 0)
    meta_row(mr).start()
    meta_v[mc] = meta[...]
    meta_v[C + mr] = meta[...]
    for b in range(RB):
        blocks[b, 0:T, :] = tok[:, b * tile:(b + 1) * tile].astype(F32)
        blocks[RB + b, 0:T, :] = cot[:, b * tile:(b + 1) * tile].astype(F32)
    pack[...] = jnp.zeros_like(pack)

    def meta_wait(k, _):
        meta_copy(k, lax.rem(mc - k + C, C), lax.rem(mc + k, C)).wait()
        return 0

    lax.fori_loop(1, C, meta_wait, 0)
    meta_row(partner).wait()
    to_smem = pltpu.make_async_copy(meta_v, meta_s, local_sem)
    to_smem.start()
    to_smem.wait()

    def a_copy(k, owner, target):
        return pltpu.make_async_remote_copy(
            src_ref=send_a.at[k], dst_ref=recv_a.at[owner], send_sem=a_send.at[k], recv_sem=a_recv.at[k],
            device_id={"col": target}, device_id_type=MESH,
        )

    def pick_for(dest):
        for s in range(3 * S):
            m = s // S
            side, base = (1, RB) if m == 2 else (0, 0)
            b = meta_s[dest, 2 * m + side, s % S] + base
            pack[s * T:(s + 1) * T, :] = blocks[b, 0:T, :]

    def a_start(k, _):
        dest = lax.rem(mc + k, C)
        pick_for(dest)
        send_a[k] = pack[...].astype(BF16)
        a_copy(k, mc, dest).start()
        return 0

    lax.fori_loop(1, C, a_start, 0)
    pick_for(mc)
    for s in range(3 * S):
        X[s, 0:T, :] = pack[s * T:(s + 1) * T, :]

    def a_wait(k, _):
        src = lax.rem(mc - k + C, C)
        a_copy(k, src, lax.rem(mc + k, C)).wait()
        pack[...] = recv_a[src].astype(F32)
        for s in range(3 * S):
            X[s, pl.ds(k * T, T), :] = pack[s * T:(s + 1) * T, :]
        return 0

    def live(m, s):
        return s < meta_s[mc, 6, m]

    def b_copy(g, m):
        return pltpu.make_async_remote_copy(
            src_ref=Pb.at[g, m], dst_ref=recv_b.at[g, m],
            send_sem=b_send.at[g, m], recv_sem=b_recv.at[g, m],
            device_id={"row": partner}, device_id_type=MESH,
        )

    def c_copy(k, owner, target):
        return pltpu.make_async_remote_copy(
            src_ref=send_c.at[k], dst_ref=got_out.at[owner], send_sem=c_send.at[k], recv_sem=c_recv.at[k],
            device_id={"col": target}, device_id_type=MESH,
        )

    def c_start(k, _):
        for s in range(3 * S):
            pack[s * T:(s + 1) * T, :] = Q[s, pl.ds(k * T, T), :]
        send_c[k] = pack[...].astype(BF16)
        c_copy(k, mc, lax.rem(mc - k + C, C)).start()
        return 0

    def forward(g):
        rows = slice(g * H, (g + 1) * H)
        lax.fori_loop(max(1, g * peers), (g + 1) * peers, a_wait, 0)
        if g == 0:
            for copy in tile_copies:
                copy.wait()
        for m in range(3):
            for s in range(S):
                part = dot(X[m * S + s, rows, :].astype(BF16), tiles_v[m, s], NT if m == 2 else NN)
                part = jnp.where(live(m, s), part, 0.0)
                P[m * S + s, rows, :] = part
                Pb[g, m, s, 0:H, :] = part.astype(BF16)
            b_copy(g, m).start()

        def place(j, _):
            for m in range(3):
                side = 0 if m == 2 else 1
                total = jnp.zeros((H, tile), F32)
                for s in range(S):
                    mine = meta_s[mc, 2 * m + side, s] == j
                    total = total + jnp.where(mine, P[m * S + s, rows, :], 0.0)
                sums[m, j, rows, :] = total
            return 0

        lax.fori_loop(0, CB, place, 0)

    def backward(g):
        rows = slice(g * H, (g + 1) * H)
        for m in range(3):
            b_copy(g, m).wait()

        def activate(j, _):
            whole = []
            for m in range(3):
                side = 0 if m == 2 else 1
                total = sums[m, j, rows, :]
                for s in range(S):
                    theirs = meta_s[C + partner, 2 * m + side, s] == j
                    total = total + jnp.where(theirs, recv_b[g, m, s, 0:H, :].astype(F32), 0.0)
                whole.append(total)
            gate, up, hg = whole
            sg = jax.nn.sigmoid(gate)
            active = gate * sg
            acts[0, j, rows, :] = hg * up * sg * (1.0 + gate * (1.0 - sg))
            acts[1, j, rows, :] = hg * active
            acts[2, j, rows, :] = active * up
            return 0

        lax.fori_loop(0, CB, activate, 0)
        for m in range(3):
            for s in range(S):
                j = meta_s[mc, 2 * m + (0 if m == 2 else 1), s]
                part = dot(acts[m, j, rows, :].astype(BF16), tiles_v[m, s], NN if m == 2 else NT)
                Q[m * S + s, rows, :] = jnp.where(live(m, s), part, 0.0)
        lax.fori_loop(max(1, g * peers), (g + 1) * peers, c_start, 0)

    for g in range(G):
        forward(g)
        if g >= 1:
            backward(g - 1)
    backward(G - 1)

    for s in range(3 * S):
        pack[s * T:(s + 1) * T, :] = Q[s, 0:T, :]
    send_c[0] = pack[...].astype(BF16)
    own_copy = pltpu.make_async_copy(send_c.at[0], got_out.at[mc], local_sem)
    own_copy.start()
    meta_out[...] = meta_v[...]

    for m in range(3):
        for s in range(S):
            j = meta_s[mc, 2 * m + (0 if m == 2 else 1), s]
            x = X[m * S + s].astype(BF16)
            act = acts[m, j].astype(BF16)
            part = dot(act, x, TN) if m == 2 else dot(x, act, TN)
            grads_v[m, s] = jnp.where(live(m, s), part, 0.0)
        grad_copies[m].start()

    def c_wait(k, _):
        src = lax.rem(mc + k, C)
        c_copy(k, src, lax.rem(mc - k + C, C)).wait()
        return 0

    lax.fori_loop(1, C, c_wait, 0)
    own_copy.wait()
    for copy in grad_copies:
        copy.wait()


def add_kernel(
    C, S, T, RB, tile, meta, got, gate_in, up_in, down_in,
    out, ingrad, gate_g, up_g, down_g, total, pack, sem,
):
    copies = [
        pltpu.make_async_copy(src, dst, sem.at[m])
        for m, (src, dst) in enumerate(((gate_in, gate_g), (up_in, up_g), (down_in, down_g)))
    ]
    for copy in copies:
        copy.start()
    total[...] = jnp.zeros_like(total)

    def add(c, _):
        pack[...] = got[c].astype(F32)
        for s in range(3 * S):
            m = s // S
            side, base = (1, RB) if m == 2 else (0, 0)
            b = meta[c, 2 * m + side, s % S] + base
            total[b, 0:T, :] += pack[s * T:(s + 1) * T, :]
        return 0

    lax.fori_loop(0, C, add, 0)
    for b in range(RB):
        ingrad[:, b * tile:(b + 1) * tile] = total[b, 0:T, :].astype(BF16)
        out[:, b * tile:(b + 1) * tile] = total[RB + b, 0:T, :].astype(BF16)
    for copy in copies:
        copy.wait()


def sparse_body(tokens, cotangent, gate_tiles, up_tiles, down_tiles, tile_index, tile_counts):
    C, R = lax.axis_size("col"), lax.axis_size("row")
    T, width = tokens.shape
    S, tile = gate_tiles.shape[0], gate_tiles.shape[-1]
    RB, CB = width // tile, FF // C // tile
    N = C * T
    rows = -(-3 * S * T // 16) * 16
    pad_t = -(-T // 8) * 8
    G = max(g for g in (1, 2, 4) if C % g == 0 and C // g * T % 8 == 0)
    padded = -(-(N // G) // 16) * 16
    meta_rows = 8
    index, counts = tile_index.transpose(0, 2, 1), tile_counts.transpose(1, 2, 0)
    V, M = pltpu.VMEM, pltpu.SemaphoreType.DMA
    vspec = pl.BlockSpec(memory_space=pltpu.VMEM)
    hbm = pl.BlockSpec(memory_space=pltpu.HBM)
    sd = jax.ShapeDtypeStruct
    got, metas, gate_grad, up_grad, down_grad = pl.pallas_call(
        functools.partial(exchange_kernel, C, S, T, RB, CB, tile, G),
        out_shape=[sd((C, rows, tile), BF16), sd((C + R, meta_rows, 128), jnp.int32)]
        + [sd((S, tile, tile), F32)] * 3,
        in_specs=[hbm] * 2 + [vspec] * 2 + [hbm] * 3,
        out_specs=[hbm, vspec] + [hbm] * 3,
        scratch_shapes=[
            V(index.shape, jnp.int32),
            V(counts.shape, jnp.int32),
            V((meta_rows, 128), jnp.int32),
            V((3, S, tile, tile), BF16),
            V((3, S, tile, tile), F32),
            V((C + R, meta_rows, 128), jnp.int32),
            pltpu.SMEM((C + R, meta_rows, 128), jnp.int32),
            V((2 * RB, pad_t, tile), F32),
            V((rows, tile), F32),
            V((C, rows, tile), BF16),
            V((C, rows, tile), BF16),
            V((3 * S, N, tile), F32),
            V((3 * S, N, tile), F32),
            V((G, 3, S, padded, tile), BF16),
            V((G, 3, S, padded, tile), BF16),
            V((3, CB, N, tile), F32),
            V((3, CB, N, tile), F32),
            V((3 * S, N, tile), F32),
            V((C, rows, tile), BF16),
            M((C,)), M((C,)), M((C,)), M((C,)), M((G, 3)), M((G, 3)), M((C,)), M((C,)),
            M((5,)), M((3,)), M,
        ],
        compiler_params=pltpu.CompilerParams(
            collective_id=0, has_side_effects=True, vmem_limit_bytes=60 * 1024 * 1024
        ),
        name="exchange",
    )(index, counts, tokens, cotangent, gate_tiles, up_tiles, down_tiles)
    return pl.pallas_call(
        functools.partial(add_kernel, C, S, T, RB, tile),
        out_shape=[sd((T, width), BF16)] * 2 + [sd((S, tile, tile), F32)] * 3,
        in_specs=[pl.BlockSpec(memory_space=pltpu.SMEM), vspec] + [hbm] * 3,
        out_specs=[vspec] * 2 + [hbm] * 3,
        scratch_shapes=[V((2 * RB, pad_t, tile), F32), V((rows, tile), F32), M((3,))],
        compiler_params=pltpu.CompilerParams(vmem_limit_bytes=60 * 1024 * 1024),
        name="add_slots",
    )(metas, got, gate_grad, up_grad, down_grad)


def solution(mesh):
    body = sparse_body if mesh.shape["row"] == 2 else dense_body
    return jax.shard_map(
        body,
        mesh=mesh,
        in_specs=(
            P("col", "row"),
            P("col", "row"),
            P("row", "col", None),
            P("row", "col", None),
            P("row", "col", None),
            P(None, "row", "col"),
            P(None, "row", "col"),
        ),
        out_specs=(
            P("col", "row"),
            P("col", "row"),
            P("row", "col", None),
            P("row", "col", None),
            P("row", "col", None),
        ),
        check_vma=False,
    )
```

```python
import functools

import jax
import jax.numpy as jnp
from jax import lax
from jax.experimental import pallas as pl
from jax.experimental.pallas import tpu as pltpu
from jax.sharding import PartitionSpec as P

FF = 16384


def pick_blocks(data_rows, block_ids, tile_size):
    token_count = data_rows.shape[0]
    block_count = data_rows.shape[1] // tile_size
    split_rows = data_rows.reshape(token_count, block_count, tile_size)
    select = (block_ids[:, None] == jnp.arange(block_count)[None, :]).astype(jnp.bfloat16)
    picked = jnp.einsum("tbk,sb->tsk", split_rows, select, preferred_element_type=jnp.float32)
    return picked.astype(jnp.bfloat16)


def place_blocks(products, block_ids, live_mask, block_count):
    select = ((block_ids[:, None] == jnp.arange(block_count)[None, :]) & live_mask[:, None]).astype(
        jnp.float32
    )
    placed = jnp.einsum("tsn,sc->tcn", products, select, precision=lax.Precision.HIGHEST)
    return placed.reshape(products.shape[0], block_count * products.shape[2])


def sparse_apply(data_rows, tiles, in_ids, out_ids, live_mask, out_count):
    picked = pick_blocks(data_rows, in_ids, tiles.shape[-1])
    products = jnp.einsum("tsk,skn->tsn", picked, tiles, preferred_element_type=jnp.float32)
    return place_blocks(products, out_ids, live_mask, out_count)


def sparse_apply_back(data_rows, tiles, in_ids, out_ids, live_mask, out_count):
    picked = pick_blocks(data_rows, in_ids, tiles.shape[-1])
    products = jnp.einsum("tsn,skn->tsk", picked, tiles, preferred_element_type=jnp.float32)
    return place_blocks(products, out_ids, live_mask, out_count)


def tile_grads(left_rows, right_rows, left_ids, right_ids, live_mask, tile_size):
    left_picked = pick_blocks(left_rows, left_ids, tile_size)
    right_picked = pick_blocks(right_rows, right_ids, tile_size)
    gradient = jnp.einsum(
        "tsk,tsn->skn", left_picked, right_picked, preferred_element_type=jnp.float32
    )
    return jnp.where(live_mask[:, None, None], gradient, jnp.zeros_like(gradient))


def gated_units(gate_sum, up_sum, hidden_grad):
    sigmoid_gate = jax.nn.sigmoid(gate_sum)
    active = gate_sum * sigmoid_gate
    hidden = (active * up_sum).astype(jnp.bfloat16)
    gate_act = (
        hidden_grad * up_sum * sigmoid_gate * (1.0 + gate_sum * (1.0 - sigmoid_gate))
    ).astype(jnp.bfloat16)
    up_act = (hidden_grad * active).astype(jnp.bfloat16)
    return (hidden, gate_act, up_act)


def dense_body(tokens, cotangent, gate_tiles, up_tiles, down_tiles, tile_index, tile_counts):
    tile_size = gate_tiles.shape[-1]
    row_blocks = tokens.shape[1] // tile_size
    col_blocks = FF // lax.axis_size("col") // tile_size
    slot_ids = jnp.arange(gate_tiles.shape[0])
    gate_live = slot_ids < tile_counts[0, 0, 0]
    up_live = slot_ids < tile_counts[1, 0, 0]
    down_live = slot_ids < tile_counts[2, 0, 0]
    gate_in, gate_out = (tile_index[0, :, 0], tile_index[0, :, 1])
    up_in, up_out = (tile_index[1, :, 0], tile_index[1, :, 1])
    down_in, down_out = (tile_index[2, :, 0], tile_index[2, :, 1])
    whole_tokens, whole_cotangent = (
        lax.all_gather(tokens, "col", axis=0, tiled=True),
        lax.all_gather(cotangent, "col", axis=0, tiled=True),
    )
    gate_part = sparse_apply(whole_tokens, gate_tiles, gate_in, gate_out, gate_live, col_blocks)
    up_part = sparse_apply(whole_tokens, up_tiles, up_in, up_out, up_live, col_blocks)
    grad_part = sparse_apply_back(
        whole_cotangent, down_tiles, down_out, down_in, down_live, col_blocks
    )
    gate_sum, up_sum, hidden_grad = (
        lax.psum_scatter(gate_part, "row", scatter_dimension=0, tiled=True),
        lax.psum_scatter(up_part, "row", scatter_dimension=0, tiled=True),
        lax.psum_scatter(grad_part, "row", scatter_dimension=0, tiled=True),
    )
    hidden, gate_act, up_act = gated_units(gate_sum, up_sum, hidden_grad)
    hidden_all, gate_all, up_all = (
        lax.all_gather(hidden, "row", axis=0, tiled=True),
        lax.all_gather(gate_act, "row", axis=0, tiled=True),
        lax.all_gather(up_act, "row", axis=0, tiled=True),
    )
    output_part = sparse_apply(hidden_all, down_tiles, down_in, down_out, down_live, row_blocks)
    input_part = sparse_apply_back(gate_all, gate_tiles, gate_out, gate_in, gate_live, row_blocks)
    input_part = input_part + sparse_apply_back(
        up_all, up_tiles, up_out, up_in, up_live, row_blocks
    )
    output_sum, input_sum = (
        lax.psum_scatter(output_part, "col", scatter_dimension=0, tiled=True),
        lax.psum_scatter(input_part, "col", scatter_dimension=0, tiled=True),
    )
    output = output_sum.astype(jnp.bfloat16)
    input_grad = input_sum.astype(jnp.bfloat16)
    gate_grad = tile_grads(whole_tokens, gate_all, gate_in, gate_out, gate_live, tile_size)
    up_grad = tile_grads(whole_tokens, up_all, up_in, up_out, up_live, tile_size)
    down_grad = tile_grads(hidden_all, whole_cotangent, down_in, down_out, down_live, tile_size)
    return (output, input_grad, gate_grad, up_grad, down_grad)


MESH = pl.DeviceIdType.MESH
F32 = jnp.float32
BF16 = jnp.bfloat16
NT = (((1,), (1,)), ((), ()))
NN = (((1,), (0,)), ((), ()))
TN = (((0,), (0,)), ((), ()))


def dot(a, b, dims):
    return lax.dot_general(a, b, dims, preferred_element_type=F32)


def exchange_kernel(
    C, S, T, RB, CB, tile, G,
    index, counts, tok, cot, gate_t, up_t, down_t,
    got_out, meta_out, gate_g, up_g, down_g,
    index_v, counts_v, meta, tiles_v, grads_v,
    meta_v, meta_s, blocks, pack, send_a, recv_a, X, P, Pb, recv_b, sums, acts, Q, send_c,
    m_send, m_recv, a_send, a_recv, b_send, b_recv, c_send, c_recv, in_sem, out_sem, local_sem,
):
    N = C * T
    H, peers = N // G, C // G
    mc, mr = lax.axis_index("col"), lax.axis_index("row")
    partner = 1 - mr
    index_copy = pltpu.make_async_copy(index, index_v, in_sem.at[3])
    counts_copy = pltpu.make_async_copy(counts, counts_v, in_sem.at[4])
    tile_copies = [
        pltpu.make_async_copy(ref, tiles_v.at[m], in_sem.at[m])
        for m, ref in enumerate((gate_t, up_t, down_t))
    ]
    grad_copies = [
        pltpu.make_async_copy(grads_v.at[m], ref, out_sem.at[m])
        for m, ref in enumerate((gate_g, up_g, down_g))
    ]
    index_copy.start()
    counts_copy.start()
    for copy in tile_copies:
        copy.start()

    barrier = pltpu.get_barrier_semaphore()

    def greet(k, _):
        pl.semaphore_signal(barrier, inc=1, device_id={"col": lax.rem(mc + k, C)}, device_id_type=MESH)
        return 0

    lax.fori_loop(1, C, greet, 0)
    pl.semaphore_signal(barrier, inc=1, device_id={"row": partner}, device_id_type=MESH)
    index_copy.wait()
    counts_copy.wait()
    meta[...] = jnp.zeros_like(meta)
    for m in range(3):
        meta[2 * m:2 * m + 2, 0:S] = index_v[m]
    meta[6:7, 0:3] = counts_v[0]
    pl.semaphore_wait(barrier, C)

    def meta_copy(k, owner, target):
        return pltpu.make_async_remote_copy(
            src_ref=meta, dst_ref=meta_v.at[owner], send_sem=m_send.at[k], recv_sem=m_recv.at[k],
            device_id={"col": target}, device_id_type=MESH,
        )

    def meta_row(owner):
        return pltpu.make_async_remote_copy(
            src_ref=meta, dst_ref=meta_v.at[C + owner], send_sem=m_send.at[0], recv_sem=m_recv.at[0],
            device_id={"row": partner}, device_id_type=MESH,
        )

    def meta_start(k, _):
        meta_copy(k, mc, lax.rem(mc + k, C)).start()
        return 0

    lax.fori_loop(1, C, meta_start, 0)
    meta_row(mr).start()
    meta_v[mc] = meta[...]
    meta_v[C + mr] = meta[...]
    for b in range(RB):
        blocks[b, 0:T, :] = tok[:, b * tile:(b + 1) * tile].astype(F32)
        blocks[RB + b, 0:T, :] = cot[:, b * tile:(b + 1) * tile].astype(F32)
    pack[...] = jnp.zeros_like(pack)

    def meta_wait(k, _):
        meta_copy(k, lax.rem(mc - k + C, C), lax.rem(mc + k, C)).wait()
        return 0

    lax.fori_loop(1, C, meta_wait, 0)
    meta_row(partner).wait()
    to_smem = pltpu.make_async_copy(meta_v, meta_s, local_sem)
    to_smem.start()
    to_smem.wait()

    def a_copy(k, owner, target):
        return pltpu.make_async_remote_copy(
            src_ref=send_a.at[k], dst_ref=recv_a.at[owner], send_sem=a_send.at[k], recv_sem=a_recv.at[k],
            device_id={"col": target}, device_id_type=MESH,
        )

    def pick_for(dest):
        for s in range(3 * S):
            m = s // S
            side, base = (1, RB) if m == 2 else (0, 0)
            b = meta_s[dest, 2 * m + side, s % S] + base
            pack[s * T:(s + 1) * T, :] = blocks[b, 0:T, :]

    def a_start(k, _):
        dest = lax.rem(mc + k, C)
        pick_for(dest)
        send_a[k] = pack[...].astype(BF16)
        a_copy(k, mc, dest).start()
        return 0

    lax.fori_loop(1, C, a_start, 0)
    pick_for(mc)
    for s in range(3 * S):
        X[s, 0:T, :] = pack[s * T:(s + 1) * T, :]

    def a_wait(k, _):
        src = lax.rem(mc - k + C, C)
        a_copy(k, src, lax.rem(mc + k, C)).wait()
        pack[...] = recv_a[src].astype(F32)
        for s in range(3 * S):
            X[s, pl.ds(k * T, T), :] = pack[s * T:(s + 1) * T, :]
        return 0

    def live(m, s):
        return s < meta_s[mc, 6, m]

    def b_copy(g, m):
        return pltpu.make_async_remote_copy(
            src_ref=Pb.at[g, m], dst_ref=recv_b.at[g, m],
            send_sem=b_send.at[g, m], recv_sem=b_recv.at[g, m],
            device_id={"row": partner}, device_id_type=MESH,
        )

    def c_copy(k, owner, target):
        return pltpu.make_async_remote_copy(
            src_ref=send_c.at[k], dst_ref=got_out.at[owner], send_sem=c_send.at[k], recv_sem=c_recv.at[k],
            device_id={"col": target}, device_id_type=MESH,
        )

    def c_start(k, _):
        for s in range(3 * S):
            pack[s * T:(s + 1) * T, :] = Q[s, pl.ds(k * T, T), :]
        send_c[k] = pack[...].astype(BF16)
        c_copy(k, mc, lax.rem(mc - k + C, C)).start()
        return 0

    def forward(g):
        rows = slice(g * H, (g + 1) * H)
        lax.fori_loop(max(1, g * peers), (g + 1) * peers, a_wait, 0)
        if g == 0:
            for copy in tile_copies:
                copy.wait()
        for m in range(3):
            for s in range(S):
                part = dot(X[m * S + s, rows, :].astype(BF16), tiles_v[m, s], NT if m == 2 else NN)
                part = jnp.where(live(m, s), part, 0.0)
                P[m * S + s, rows, :] = part
                Pb[g, m, s, 0:H, :] = part.astype(BF16)
            b_copy(g, m).start()

        def place(j, _):
            for m in range(3):
                side = 0 if m == 2 else 1
                total = jnp.zeros((H, tile), F32)
                for s in range(S):
                    mine = meta_s[mc, 2 * m + side, s] == j
                    total = total + jnp.where(mine, P[m * S + s, rows, :], 0.0)
                sums[m, j, rows, :] = total
            return 0

        lax.fori_loop(0, CB, place, 0)

    def backward(g):
        rows = slice(g * H, (g + 1) * H)
        for m in range(3):
            b_copy(g, m).wait()

        def activate(j, _):
            whole = []
            for m in range(3):
                side = 0 if m == 2 else 1
                total = sums[m, j, rows, :]
                for s in range(S):
                    theirs = meta_s[C + partner, 2 * m + side, s] == j
                    total = total + jnp.where(theirs, recv_b[g, m, s, 0:H, :].astype(F32), 0.0)
                whole.append(total)
            gate, up, hg = whole
            sg = jax.nn.sigmoid(gate)
            active = gate * sg
            acts[0, j, rows, :] = hg * up * sg * (1.0 + gate * (1.0 - sg))
            acts[1, j, rows, :] = hg * active
            acts[2, j, rows, :] = active * up
            return 0

        lax.fori_loop(0, CB, activate, 0)
        for m in range(3):
            for s in range(S):
                j = meta_s[mc, 2 * m + (0 if m == 2 else 1), s]
                part = dot(acts[m, j, rows, :].astype(BF16), tiles_v[m, s], NN if m == 2 else NT)
                Q[m * S + s, rows, :] = jnp.where(live(m, s), part, 0.0)
        lax.fori_loop(max(1, g * peers), (g + 1) * peers, c_start, 0)

    for g in range(G):
        forward(g)
        if g >= 1:
            backward(g - 1)
    backward(G - 1)

    for s in range(3 * S):
        pack[s * T:(s + 1) * T, :] = Q[s, 0:T, :]
    send_c[0] = pack[...].astype(BF16)
    own_copy = pltpu.make_async_copy(send_c.at[0], got_out.at[mc], local_sem)
    own_copy.start()
    meta_out[...] = meta_v[...]

    for m in range(3):
        for s in range(S):
            j = meta_s[mc, 2 * m + (0 if m == 2 else 1), s]
            x = X[m * S + s].astype(BF16)
            act = acts[m, j].astype(BF16)
            part = dot(act, x, TN) if m == 2 else dot(x, act, TN)
            grads_v[m, s] = jnp.where(live(m, s), part, 0.0)
        grad_copies[m].start()

    def c_wait(k, _):
        src = lax.rem(mc + k, C)
        c_copy(k, src, lax.rem(mc - k + C, C)).wait()
        return 0

    lax.fori_loop(1, C, c_wait, 0)
    own_copy.wait()
    for copy in grad_copies:
        copy.wait()


def add_kernel(
    C, S, T, RB, tile, meta, got, gate_in, up_in, down_in,
    out, ingrad, gate_g, up_g, down_g, total, pack, held, load_sem, store_sem,
):
    loads = [
        pltpu.make_async_copy(src, held.at[m], load_sem.at[m])
        for m, src in enumerate((gate_in, up_in, down_in))
    ]
    stores = [
        pltpu.make_async_copy(held.at[m], dst, store_sem.at[m])
        for m, dst in enumerate((gate_g, up_g, down_g))
    ]
    for copy in loads:
        copy.start()
    total[...] = jnp.zeros_like(total)

    def add(c, _):
        pack[...] = got[c].astype(F32)
        for s in range(3 * S):
            m = s // S
            side, base = (1, RB) if m == 2 else (0, 0)
            b = meta[c, 2 * m + side, s % S] + base
            total[b, 0:T, :] += pack[s * T:(s + 1) * T, :]
        return 0

    lax.fori_loop(0, C, add, 0)
    for load, store in zip(loads, stores):
        load.wait()
        store.start()
    for b in range(RB):
        ingrad[:, b * tile:(b + 1) * tile] = total[b, 0:T, :].astype(BF16)
        out[:, b * tile:(b + 1) * tile] = total[RB + b, 0:T, :].astype(BF16)
    for store in stores:
        store.wait()


def sparse_body(tokens, cotangent, gate_tiles, up_tiles, down_tiles, tile_index, tile_counts):
    C, R = lax.axis_size("col"), lax.axis_size("row")
    T, width = tokens.shape
    S, tile = gate_tiles.shape[0], gate_tiles.shape[-1]
    RB, CB = width // tile, FF // C // tile
    N = C * T
    rows = -(-3 * S * T // 16) * 16
    pad_t = -(-T // 8) * 8
    G = max(g for g in (1, 2, 4) if C % g == 0 and C // g * T % 8 == 0)
    padded = -(-(N // G) // 16) * 16
    meta_rows = 8
    index, counts = tile_index.transpose(0, 2, 1), tile_counts.transpose(1, 2, 0)
    V, M = pltpu.VMEM, pltpu.SemaphoreType.DMA
    vspec = pl.BlockSpec(memory_space=pltpu.VMEM)
    hbm = pl.BlockSpec(memory_space=pltpu.HBM)
    sd = jax.ShapeDtypeStruct
    got, metas, gate_grad, up_grad, down_grad = pl.pallas_call(
        functools.partial(exchange_kernel, C, S, T, RB, CB, tile, G),
        out_shape=[sd((C, rows, tile), BF16), sd((C + R, meta_rows, 128), jnp.int32)]
        + [sd((S, tile, tile), F32)] * 3,
        in_specs=[hbm] * 2 + [vspec] * 2 + [hbm] * 3,
        out_specs=[hbm, vspec] + [hbm] * 3,
        scratch_shapes=[
            V(index.shape, jnp.int32),
            V(counts.shape, jnp.int32),
            V((meta_rows, 128), jnp.int32),
            V((3, S, tile, tile), BF16),
            V((3, S, tile, tile), F32),
            V((C + R, meta_rows, 128), jnp.int32),
            pltpu.SMEM((C + R, meta_rows, 128), jnp.int32),
            V((2 * RB, pad_t, tile), F32),
            V((rows, tile), F32),
            V((C, rows, tile), BF16),
            V((C, rows, tile), BF16),
            V((3 * S, N, tile), F32),
            V((3 * S, N, tile), F32),
            V((G, 3, S, padded, tile), BF16),
            V((G, 3, S, padded, tile), BF16),
            V((3, CB, N, tile), F32),
            V((3, CB, N, tile), F32),
            V((3 * S, N, tile), F32),
            V((C, rows, tile), BF16),
            M((C,)), M((C,)), M((C,)), M((C,)), M((G, 3)), M((G, 3)), M((C,)), M((C,)),
            M((5,)), M((3,)), M,
        ],
        compiler_params=pltpu.CompilerParams(
            collective_id=0, has_side_effects=True, vmem_limit_bytes=60 * 1024 * 1024
        ),
        name="exchange",
    )(index, counts, tokens, cotangent, gate_tiles, up_tiles, down_tiles)
    return pl.pallas_call(
        functools.partial(add_kernel, C, S, T, RB, tile),
        out_shape=[sd((T, width), BF16)] * 2 + [sd((S, tile, tile), F32)] * 3,
        in_specs=[pl.BlockSpec(memory_space=pltpu.SMEM), vspec] + [hbm] * 3,
        out_specs=[vspec] * 2 + [hbm] * 3,
        scratch_shapes=[
            V((2 * RB, pad_t, tile), F32), V((rows, tile), F32),
            V((3, S, tile, tile), F32), M((3,)), M((3,)),
        ],
        compiler_params=pltpu.CompilerParams(vmem_limit_bytes=60 * 1024 * 1024),
        name="add_slots",
    )(metas, got, gate_grad, up_grad, down_grad)


def solution(mesh):
    body = sparse_body if mesh.shape["row"] == 2 else dense_body
    return jax.shard_map(
        body,
        mesh=mesh,
        in_specs=(
            P("col", "row"),
            P("col", "row"),
            P("row", "col", None),
            P("row", "col", None),
            P("row", "col", None),
            P(None, "row", "col"),
            P(None, "row", "col"),
        ),
        out_specs=(
            P("col", "row"),
            P("col", "row"),
            P("row", "col", None),
            P("row", "col", None),
            P("row", "col", None),
        ),
        check_vma=False,
    )
```

```python
import functools

import jax
import jax.numpy as jnp
from jax import lax
from jax.experimental import pallas as pl
from jax.experimental.pallas import tpu as pltpu
from jax.sharding import PartitionSpec as P

FF = 16384


def pick_blocks(data_rows, block_ids, tile_size):
    token_count = data_rows.shape[0]
    block_count = data_rows.shape[1] // tile_size
    split_rows = data_rows.reshape(token_count, block_count, tile_size)
    select = (block_ids[:, None] == jnp.arange(block_count)[None, :]).astype(jnp.bfloat16)
    picked = jnp.einsum("tbk,sb->tsk", split_rows, select, preferred_element_type=jnp.float32)
    return picked.astype(jnp.bfloat16)


def place_blocks(products, block_ids, live_mask, block_count):
    select = ((block_ids[:, None] == jnp.arange(block_count)[None, :]) & live_mask[:, None]).astype(
        jnp.float32
    )
    placed = jnp.einsum("tsn,sc->tcn", products, select, precision=lax.Precision.HIGHEST)
    return placed.reshape(products.shape[0], block_count * products.shape[2])


def sparse_apply(data_rows, tiles, in_ids, out_ids, live_mask, out_count):
    picked = pick_blocks(data_rows, in_ids, tiles.shape[-1])
    products = jnp.einsum("tsk,skn->tsn", picked, tiles, preferred_element_type=jnp.float32)
    return place_blocks(products, out_ids, live_mask, out_count)


def sparse_apply_back(data_rows, tiles, in_ids, out_ids, live_mask, out_count):
    picked = pick_blocks(data_rows, in_ids, tiles.shape[-1])
    products = jnp.einsum("tsn,skn->tsk", picked, tiles, preferred_element_type=jnp.float32)
    return place_blocks(products, out_ids, live_mask, out_count)


def tile_grads(left_rows, right_rows, left_ids, right_ids, live_mask, tile_size):
    left_picked = pick_blocks(left_rows, left_ids, tile_size)
    right_picked = pick_blocks(right_rows, right_ids, tile_size)
    gradient = jnp.einsum(
        "tsk,tsn->skn", left_picked, right_picked, preferred_element_type=jnp.float32
    )
    return jnp.where(live_mask[:, None, None], gradient, jnp.zeros_like(gradient))


def gated_units(gate_sum, up_sum, hidden_grad):
    sigmoid_gate = jax.nn.sigmoid(gate_sum)
    active = gate_sum * sigmoid_gate
    hidden = (active * up_sum).astype(jnp.bfloat16)
    gate_act = (
        hidden_grad * up_sum * sigmoid_gate * (1.0 + gate_sum * (1.0 - sigmoid_gate))
    ).astype(jnp.bfloat16)
    up_act = (hidden_grad * active).astype(jnp.bfloat16)
    return (hidden, gate_act, up_act)


def dense_body(tokens, cotangent, gate_tiles, up_tiles, down_tiles, tile_index, tile_counts):
    tile_size = gate_tiles.shape[-1]
    row_blocks = tokens.shape[1] // tile_size
    col_blocks = FF // lax.axis_size("col") // tile_size
    slot_ids = jnp.arange(gate_tiles.shape[0])
    gate_live = slot_ids < tile_counts[0, 0, 0]
    up_live = slot_ids < tile_counts[1, 0, 0]
    down_live = slot_ids < tile_counts[2, 0, 0]
    gate_in, gate_out = (tile_index[0, :, 0], tile_index[0, :, 1])
    up_in, up_out = (tile_index[1, :, 0], tile_index[1, :, 1])
    down_in, down_out = (tile_index[2, :, 0], tile_index[2, :, 1])
    whole_tokens, whole_cotangent = (
        lax.all_gather(tokens, "col", axis=0, tiled=True),
        lax.all_gather(cotangent, "col", axis=0, tiled=True),
    )
    gate_part = sparse_apply(whole_tokens, gate_tiles, gate_in, gate_out, gate_live, col_blocks)
    up_part = sparse_apply(whole_tokens, up_tiles, up_in, up_out, up_live, col_blocks)
    grad_part = sparse_apply_back(
        whole_cotangent, down_tiles, down_out, down_in, down_live, col_blocks
    )
    gate_sum, up_sum, hidden_grad = (
        lax.psum_scatter(gate_part, "row", scatter_dimension=0, tiled=True),
        lax.psum_scatter(up_part, "row", scatter_dimension=0, tiled=True),
        lax.psum_scatter(grad_part, "row", scatter_dimension=0, tiled=True),
    )
    hidden, gate_act, up_act = gated_units(gate_sum, up_sum, hidden_grad)
    hidden_all, gate_all, up_all = (
        lax.all_gather(hidden, "row", axis=0, tiled=True),
        lax.all_gather(gate_act, "row", axis=0, tiled=True),
        lax.all_gather(up_act, "row", axis=0, tiled=True),
    )
    output_part = sparse_apply(hidden_all, down_tiles, down_in, down_out, down_live, row_blocks)
    input_part = sparse_apply_back(gate_all, gate_tiles, gate_out, gate_in, gate_live, row_blocks)
    input_part = input_part + sparse_apply_back(
        up_all, up_tiles, up_out, up_in, up_live, row_blocks
    )
    output_sum, input_sum = (
        lax.psum_scatter(output_part, "col", scatter_dimension=0, tiled=True),
        lax.psum_scatter(input_part, "col", scatter_dimension=0, tiled=True),
    )
    output = output_sum.astype(jnp.bfloat16)
    input_grad = input_sum.astype(jnp.bfloat16)
    gate_grad = tile_grads(whole_tokens, gate_all, gate_in, gate_out, gate_live, tile_size)
    up_grad = tile_grads(whole_tokens, up_all, up_in, up_out, up_live, tile_size)
    down_grad = tile_grads(hidden_all, whole_cotangent, down_in, down_out, down_live, tile_size)
    return (output, input_grad, gate_grad, up_grad, down_grad)


MESH = pl.DeviceIdType.MESH
PLANE = 4
F32 = jnp.float32
BF16 = jnp.bfloat16
NT = (((1,), (1,)), ((), ()))
NN = (((1,), (0,)), ((), ()))
TN = (((0,), (0,)), ((), ()))


def dot(a, b, dims):
    return lax.dot_general(a, b, dims, preferred_element_type=F32)


def exchange_kernel(
    C, S, T, RB, CB, tile, G,
    index, counts, tok, cot, gate_t, up_t, down_t,
    got_out, meta_out, gate_g, up_g, down_g,
    index_v, counts_v, meta, tiles_v, grads_v, flat, dense,
    meta_v, meta_s, blocks, pack, send_a, recv_a, X, P, Pb, recv_b, sums, acts, Q, send_c,
    m_send, m_recv, a_send, a_recv, b_send, b_recv, c_send, c_recv, l_send, l_recv, in_sem, out_sem,
    local_sem, save_sem,
):
    N = C * T
    H = N // G
    mc, mr = lax.axis_index("col"), lax.axis_index("row")
    partner = 1 - mr
    index_copy = pltpu.make_async_copy(index, index_v, in_sem.at[3])
    counts_copy = pltpu.make_async_copy(counts, counts_v, in_sem.at[4])
    tile_copies = [
        pltpu.make_async_copy(ref, tiles_v.at[m], in_sem.at[m])
        for m, ref in enumerate((gate_t, up_t, down_t))
    ]
    grad_copies = [
        pltpu.make_async_copy(grads_v.at[m], ref, out_sem.at[m])
        for m, ref in enumerate((gate_g, up_g, down_g))
    ]
    index_copy.start()
    counts_copy.start()
    for copy in tile_copies:
        copy.start()

    barrier = pltpu.get_barrier_semaphore()

    def greet(k, _):
        pl.semaphore_signal(barrier, inc=1, device_id={"col": lax.rem(mc + k, C)}, device_id_type=MESH)
        return 0

    lax.fori_loop(1, C, greet, 0)
    pl.semaphore_signal(barrier, inc=1, device_id={"row": partner}, device_id_type=MESH)
    index_copy.wait()
    counts_copy.wait()
    meta[...] = jnp.zeros_like(meta)
    for m in range(3):
        meta[2 * m:2 * m + 2, 0:S] = index_v[m]
    meta[6:7, 0:3] = counts_v[0]
    for b in range(RB):
        flat[b * T:(b + 1) * T, :] = tok[:, b * tile:(b + 1) * tile].astype(F32)
        flat[(RB + b) * T:(RB + b + 1) * T, :] = cot[:, b * tile:(b + 1) * tile].astype(F32)
    pl.semaphore_wait(barrier, C)

    line, here = C // PLANE, lax.rem(mc, PLANE)
    z = lax.div(mc, PLANE)

    def ahead(k):
        return lax.rem(mc + k, C)

    def behind(k):
        return lax.rem(mc - k + C, C)

    def peer(q):
        return z * PLANE + lax.rem(here + q, PLANE)

    def source(q):
        return lax.rem(here - q + PLANE, PLANE)

    def meta_copy(k, owner):
        return pltpu.make_async_remote_copy(
            src_ref=meta, dst_ref=meta_v.at[owner], send_sem=m_send.at[k], recv_sem=m_recv.at[k],
            device_id={"col": ahead(k)}, device_id_type=MESH,
        )

    def meta_row(owner):
        return pltpu.make_async_remote_copy(
            src_ref=meta, dst_ref=meta_v.at[C + owner], send_sem=m_send.at[0], recv_sem=m_recv.at[0],
            device_id={"row": partner}, device_id_type=MESH,
        )

    def line_copy(origin, up):
        return pltpu.make_async_remote_copy(
            src_ref=dense.at[origin], dst_ref=dense.at[origin],
            send_sem=l_send.at[origin, up], recv_sem=l_recv.at[origin],
            device_id={"col": mc + PLANE if up else mc - PLANE}, device_id_type=MESH,
        )

    for k in range(1, PLANE):
        meta_copy(k, mc).start()
    dense[z] = flat[...].astype(BF16)

    @pl.when(z < line - 1)
    def _():
        line_copy(z, 1).start()

    @pl.when(z > 0)
    def _():
        line_copy(z, 0).start()

    for k in range(PLANE, C):
        meta_copy(k, mc).start()
    meta_row(mr).start()
    meta_v[mc] = meta[...]
    meta_v[C + mr] = meta[...]
    pack[...] = jnp.zeros_like(pack)
    for k in range(1, C):
        meta_copy(k, behind(k)).wait()
    meta_row(partner).wait()
    to_smem = pltpu.make_async_copy(meta_v, meta_s, local_sem)
    to_smem.start()
    to_smem.wait()
    meta_save = pltpu.make_async_copy(meta_v, meta_out, save_sem)
    meta_save.start()

    def origin_of(t):
        half = lax.div(z, 2)
        return (z, z + 1 - 2 * lax.rem(z, 2), 2 - half, 3 - 3 * half)[t]

    def a_copy(t, q, owner):
        return pltpu.make_async_remote_copy(
            src_ref=send_a.at[t, q], dst_ref=recv_a.at[t, owner],
            send_sem=a_send.at[t, q], recv_sem=a_recv.at[t, q],
            device_id={"col": peer(q)}, device_id_type=MESH,
        )

    def pick_for(dest):
        for s in range(3 * S):
            m = s // S
            side, base = (1, RB) if m == 2 else (0, 0)
            b = meta_s[dest, 2 * m + side, s % S] + base
            pack[s * T:(s + 1) * T, :] = blocks[b, 0:T, :]

    def stage(t):
        if t > 0:
            origin = origin_of(t)
            line_copy(origin, 0).wait_recv()

            @pl.when((origin < z) & (z < line - 1))
            def _():
                line_copy(origin, 1).start()

            @pl.when((origin > z) & (z > 0))
            def _():
                line_copy(origin, 0).start()

            flat[...] = dense[origin].astype(F32)
        for b in range(2 * RB):
            blocks[b, 0:T, :] = flat[b * T:(b + 1) * T, :]

        def send(q, _):
            pick_for(peer(q))
            send_a[t, q] = pack[...].astype(BF16)
            a_copy(t, q, here).start()
            return 0

        lax.fori_loop(1, PLANE, send, 0)
        pick_for(mc)
        for s in range(3 * S):
            X[s, t * PLANE * T:t * PLANE * T + T, :] = pack[s * T:(s + 1) * T, :]

    def a_wait(t):
        for q in range(1, PLANE):
            a_copy(t, q, source(q)).wait()
            pack[...] = recv_a[t, source(q)].astype(F32)
            at = (t * PLANE + q) * T
            for s in range(3 * S):
                X[s, at:at + T, :] = pack[s * T:(s + 1) * T, :]

    def live(m, s):
        return s < meta_s[mc, 6, m]

    def b_copy(g, m):
        return pltpu.make_async_remote_copy(
            src_ref=Pb.at[g, m], dst_ref=recv_b.at[g, m],
            send_sem=b_send.at[g, m], recv_sem=b_recv.at[g, m],
            device_id={"row": partner}, device_id_type=MESH,
        )

    def c_copy(k, dest, owner, turn):
        return pltpu.make_async_remote_copy(
            src_ref=send_c.at[k], dst_ref=got_out.at[owner],
            send_sem=c_send.at[k], recv_sem=c_recv.at[turn],
            device_id={"col": dest}, device_id_type=MESH,
        )

    def c_pack(k):
        for s in range(3 * S):
            pack[s * T:(s + 1) * T, :] = Q[s, k * T:(k + 1) * T, :]
        send_c[k] = pack[...].astype(BF16)

    def c_dest(k):
        return origin_of(k // PLANE) * PLANE + source(k % PLANE)

    own_copy = pltpu.make_async_copy(send_c.at[0], got_out.at[mc], local_sem)

    def c_start(k):
        c_pack(k)
        if k == 0:
            own_copy.start()
        else:
            c_copy(k, c_dest(k), mc, lax.rem(mc - c_dest(k) + C, C)).start()

    def forward(g):
        rows = slice(g * H, (g + 1) * H)
        a_wait(g)
        if g == 0:
            for copy in tile_copies:
                copy.wait()
        for m in range(3):
            for s in range(S):
                part = dot(X[m * S + s, rows, :].astype(BF16), tiles_v[m, s], NT if m == 2 else NN)
                part = jnp.where(live(m, s), part, 0.0)
                P[m * S + s, rows, :] = part
                Pb[g, m, s, 0:H, :] = part.astype(BF16)
            b_copy(g, m).start()

        def place(j, _):
            for m in range(3):
                side = 0 if m == 2 else 1
                total = jnp.zeros((H, tile), F32)
                for s in range(S):
                    mine = meta_s[mc, 2 * m + side, s] == j
                    total = total + jnp.where(mine, P[m * S + s, rows, :], 0.0)
                sums[m, j, rows, :] = total
            return 0

        lax.fori_loop(0, CB, place, 0)

    def backward(g):
        rows = slice(g * H, (g + 1) * H)
        for m in range(3):
            b_copy(g, m).wait()

        def activate(j, _):
            whole = []
            for m in range(3):
                side = 0 if m == 2 else 1
                total = sums[m, j, rows, :]
                for s in range(S):
                    theirs = meta_s[C + partner, 2 * m + side, s] == j
                    total = total + jnp.where(theirs, recv_b[g, m, s, 0:H, :].astype(F32), 0.0)
                whole.append(total)
            gate, up, hg = whole
            sg = jax.nn.sigmoid(gate)
            active = gate * sg
            acts[0, j, rows, :] = hg * up * sg * (1.0 + gate * (1.0 - sg))
            acts[1, j, rows, :] = hg * active
            acts[2, j, rows, :] = active * up
            return 0

        lax.fori_loop(0, CB, activate, 0)
        for m in range(3):
            for s in range(S):
                j = meta_s[mc, 2 * m + (0 if m == 2 else 1), s]
                part = dot(acts[m, j, rows, :].astype(BF16), tiles_v[m, s], NN if m == 2 else NT)
                Q[m * S + s, rows, :] = jnp.where(live(m, s), part, 0.0)
        for k in range(g * PLANE, (g + 1) * PLANE):
            c_start(k)

    stage(0)
    for g in range(G):
        if g + 1 < G:
            stage(g + 1)
        forward(g)
        if g >= 1:
            backward(g - 1)
    backward(G - 1)

    for m in range(3):
        for s in range(S):
            j = meta_s[mc, 2 * m + (0 if m == 2 else 1), s]
            x = X[m * S + s].astype(BF16)
            act = acts[m, j].astype(BF16)
            part = dot(act, x, TN) if m == 2 else dot(x, act, TN)
            grads_v[m, s] = jnp.where(live(m, s), part, 0.0)
        grad_copies[m].start()

    for k in range(1, C):
        dest = c_dest(k)
        c_copy(k, dest, dest, lax.rem(dest - mc + C, C)).wait()
    for t in range(line):
        origin = origin_of(t)

        @pl.when((origin <= z) & (z < line - 1))
        def _():
            line_copy(origin, 1).wait_send()

        @pl.when((origin >= z) & (z > 0))
        def _():
            line_copy(origin, 0).wait_send()

    meta_save.wait()
    own_copy.wait()
    for copy in grad_copies:
        copy.wait()


def add_kernel(
    C, S, T, RB, tile, meta, got, gate_in, up_in, down_in,
    out, ingrad, gate_g, up_g, down_g, total, pack, held, load_sem, store_sem,
):
    loads = [
        pltpu.make_async_copy(src, held.at[m], load_sem.at[m])
        for m, src in enumerate((gate_in, up_in, down_in))
    ]
    stores = [
        pltpu.make_async_copy(held.at[m], dst, store_sem.at[m])
        for m, dst in enumerate((gate_g, up_g, down_g))
    ]
    for copy in loads:
        copy.start()
    total[...] = jnp.zeros_like(total)

    def add(c, _):
        pack[...] = got[c].astype(F32)
        for s in range(3 * S):
            m = s // S
            side, base = (1, RB) if m == 2 else (0, 0)
            b = meta[c, 2 * m + side, s % S] + base
            total[b, 0:T, :] += pack[s * T:(s + 1) * T, :]
        return 0

    lax.fori_loop(0, C, add, 0)
    for load, store in zip(loads, stores):
        load.wait()
        store.start()
    for b in range(RB):
        ingrad[:, b * tile:(b + 1) * tile] = total[b, 0:T, :].astype(BF16)
        out[:, b * tile:(b + 1) * tile] = total[RB + b, 0:T, :].astype(BF16)
    for store in stores:
        store.wait()


def sparse_body(tokens, cotangent, gate_tiles, up_tiles, down_tiles, tile_index, tile_counts):
    C, R = lax.axis_size("col"), lax.axis_size("row")
    T, width = tokens.shape
    S, tile = gate_tiles.shape[0], gate_tiles.shape[-1]
    RB, CB = width // tile, FF // C // tile
    N = C * T
    rows = -(-3 * S * T // 16) * 16
    pad_t = -(-T // 8) * 8
    G = C // PLANE
    padded = -(-(N // G) // 16) * 16
    meta_rows = 8
    index, counts = tile_index.transpose(0, 2, 1), tile_counts.transpose(1, 2, 0)
    V, M = pltpu.VMEM, pltpu.SemaphoreType.DMA
    vspec = pl.BlockSpec(memory_space=pltpu.VMEM)
    hbm = pl.BlockSpec(memory_space=pltpu.HBM)
    sd = jax.ShapeDtypeStruct
    got, metas, gate_grad, up_grad, down_grad = pl.pallas_call(
        functools.partial(exchange_kernel, C, S, T, RB, CB, tile, G),
        out_shape=[sd((C, rows, tile), BF16), sd((C + R, meta_rows, 128), jnp.int32)]
        + [sd((S, tile, tile), F32)] * 3,
        in_specs=[hbm] * 2 + [vspec] * 2 + [hbm] * 3,
        out_specs=[hbm] * 5,
        scratch_shapes=[
            V(index.shape, jnp.int32),
            V(counts.shape, jnp.int32),
            V((meta_rows, 128), jnp.int32),
            V((3, S, tile, tile), BF16),
            V((3, S, tile, tile), F32),
            V((2 * RB * T, tile), F32),
            V((G, 2 * RB * T, tile), BF16),
            V((C + R, meta_rows, 128), jnp.int32),
            pltpu.SMEM((C + R, meta_rows, 128), jnp.int32),
            V((2 * RB, pad_t, tile), F32),
            V((rows, tile), F32),
            V((G, PLANE, rows, tile), BF16),
            V((G, PLANE, rows, tile), BF16),
            V((3 * S, N, tile), F32),
            V((3 * S, N, tile), F32),
            V((G, 3, S, padded, tile), BF16),
            V((G, 3, S, padded, tile), BF16),
            V((3, CB, N, tile), F32),
            V((3, CB, N, tile), F32),
            V((3 * S, N, tile), F32),
            V((C, rows, tile), BF16),
            M((C,)), M((C,)), M((G, PLANE)), M((G, PLANE)), M((G, 3)), M((G, 3)), M((C,)), M((C,)),
            M((G, 2)), M((G,)), M((5,)), M((3,)), M, M,
        ],
        compiler_params=pltpu.CompilerParams(
            collective_id=0, has_side_effects=True, vmem_limit_bytes=60 * 1024 * 1024
        ),
        name="exchange",
    )(index, counts, tokens, cotangent, gate_tiles, up_tiles, down_tiles)
    return pl.pallas_call(
        functools.partial(add_kernel, C, S, T, RB, tile),
        out_shape=[sd((T, width), BF16)] * 2 + [sd((S, tile, tile), F32)] * 3,
        in_specs=[pl.BlockSpec(memory_space=pltpu.SMEM), vspec] + [hbm] * 3,
        out_specs=[vspec] * 2 + [hbm] * 3,
        scratch_shapes=[
            V((2 * RB, pad_t, tile), F32), V((rows, tile), F32),
            V((3, S, tile, tile), F32), M((3,)), M((3,)),
        ],
        compiler_params=pltpu.CompilerParams(vmem_limit_bytes=60 * 1024 * 1024),
        name="add_slots",
    )(metas, got, gate_grad, up_grad, down_grad)


def solution(mesh):
    body = sparse_body if (mesh.shape["row"], mesh.shape["col"]) == (2, 4 * PLANE) else dense_body
    return jax.shard_map(
        body,
        mesh=mesh,
        in_specs=(
            P("col", "row"),
            P("col", "row"),
            P("row", "col", None),
            P("row", "col", None),
            P("row", "col", None),
            P(None, "row", "col"),
            P(None, "row", "col"),
        ),
        out_specs=(
            P("col", "row"),
            P("col", "row"),
            P("row", "col", None),
            P("row", "col", None),
            P("row", "col", None),
        ),
        check_vma=False,
    )
```

```python
import functools

import jax
import jax.numpy as jnp
from jax import lax
from jax.experimental import pallas as pl
from jax.experimental.pallas import tpu as pltpu
from jax.sharding import PartitionSpec as P

FF = 16384


def pick_blocks(data_rows, block_ids, tile_size):
    token_count = data_rows.shape[0]
    block_count = data_rows.shape[1] // tile_size
    split_rows = data_rows.reshape(token_count, block_count, tile_size)
    select = (block_ids[:, None] == jnp.arange(block_count)[None, :]).astype(jnp.bfloat16)
    picked = jnp.einsum("tbk,sb->tsk", split_rows, select, preferred_element_type=jnp.float32)
    return picked.astype(jnp.bfloat16)


def place_blocks(products, block_ids, live_mask, block_count):
    select = ((block_ids[:, None] == jnp.arange(block_count)[None, :]) & live_mask[:, None]).astype(
        jnp.float32
    )
    placed = jnp.einsum("tsn,sc->tcn", products, select, precision=lax.Precision.HIGHEST)
    return placed.reshape(products.shape[0], block_count * products.shape[2])


def sparse_apply(data_rows, tiles, in_ids, out_ids, live_mask, out_count):
    picked = pick_blocks(data_rows, in_ids, tiles.shape[-1])
    products = jnp.einsum("tsk,skn->tsn", picked, tiles, preferred_element_type=jnp.float32)
    return place_blocks(products, out_ids, live_mask, out_count)


def sparse_apply_back(data_rows, tiles, in_ids, out_ids, live_mask, out_count):
    picked = pick_blocks(data_rows, in_ids, tiles.shape[-1])
    products = jnp.einsum("tsn,skn->tsk", picked, tiles, preferred_element_type=jnp.float32)
    return place_blocks(products, out_ids, live_mask, out_count)


def tile_grads(left_rows, right_rows, left_ids, right_ids, live_mask, tile_size):
    left_picked = pick_blocks(left_rows, left_ids, tile_size)
    right_picked = pick_blocks(right_rows, right_ids, tile_size)
    gradient = jnp.einsum(
        "tsk,tsn->skn", left_picked, right_picked, preferred_element_type=jnp.float32
    )
    return jnp.where(live_mask[:, None, None], gradient, jnp.zeros_like(gradient))


def gated_units(gate_sum, up_sum, hidden_grad):
    sigmoid_gate = jax.nn.sigmoid(gate_sum)
    active = gate_sum * sigmoid_gate
    hidden = (active * up_sum).astype(jnp.bfloat16)
    gate_act = (
        hidden_grad * up_sum * sigmoid_gate * (1.0 + gate_sum * (1.0 - sigmoid_gate))
    ).astype(jnp.bfloat16)
    up_act = (hidden_grad * active).astype(jnp.bfloat16)
    return (hidden, gate_act, up_act)


def dense_body(tokens, cotangent, gate_tiles, up_tiles, down_tiles, tile_index, tile_counts):
    tile_size = gate_tiles.shape[-1]
    row_blocks = tokens.shape[1] // tile_size
    col_blocks = FF // lax.axis_size("col") // tile_size
    slot_ids = jnp.arange(gate_tiles.shape[0])
    gate_live = slot_ids < tile_counts[0, 0, 0]
    up_live = slot_ids < tile_counts[1, 0, 0]
    down_live = slot_ids < tile_counts[2, 0, 0]
    gate_in, gate_out = (tile_index[0, :, 0], tile_index[0, :, 1])
    up_in, up_out = (tile_index[1, :, 0], tile_index[1, :, 1])
    down_in, down_out = (tile_index[2, :, 0], tile_index[2, :, 1])
    whole_tokens, whole_cotangent = (
        lax.all_gather(tokens, "col", axis=0, tiled=True),
        lax.all_gather(cotangent, "col", axis=0, tiled=True),
    )
    gate_part = sparse_apply(whole_tokens, gate_tiles, gate_in, gate_out, gate_live, col_blocks)
    up_part = sparse_apply(whole_tokens, up_tiles, up_in, up_out, up_live, col_blocks)
    grad_part = sparse_apply_back(
        whole_cotangent, down_tiles, down_out, down_in, down_live, col_blocks
    )
    gate_sum, up_sum, hidden_grad = (
        lax.psum_scatter(gate_part, "row", scatter_dimension=0, tiled=True),
        lax.psum_scatter(up_part, "row", scatter_dimension=0, tiled=True),
        lax.psum_scatter(grad_part, "row", scatter_dimension=0, tiled=True),
    )
    hidden, gate_act, up_act = gated_units(gate_sum, up_sum, hidden_grad)
    hidden_all, gate_all, up_all = (
        lax.all_gather(hidden, "row", axis=0, tiled=True),
        lax.all_gather(gate_act, "row", axis=0, tiled=True),
        lax.all_gather(up_act, "row", axis=0, tiled=True),
    )
    output_part = sparse_apply(hidden_all, down_tiles, down_in, down_out, down_live, row_blocks)
    input_part = sparse_apply_back(gate_all, gate_tiles, gate_out, gate_in, gate_live, row_blocks)
    input_part = input_part + sparse_apply_back(
        up_all, up_tiles, up_out, up_in, up_live, row_blocks
    )
    output_sum, input_sum = (
        lax.psum_scatter(output_part, "col", scatter_dimension=0, tiled=True),
        lax.psum_scatter(input_part, "col", scatter_dimension=0, tiled=True),
    )
    output = output_sum.astype(jnp.bfloat16)
    input_grad = input_sum.astype(jnp.bfloat16)
    gate_grad = tile_grads(whole_tokens, gate_all, gate_in, gate_out, gate_live, tile_size)
    up_grad = tile_grads(whole_tokens, up_all, up_in, up_out, up_live, tile_size)
    down_grad = tile_grads(hidden_all, whole_cotangent, down_in, down_out, down_live, tile_size)
    return (output, input_grad, gate_grad, up_grad, down_grad)


MESH = pl.DeviceIdType.MESH
F32 = jnp.float32
BF16 = jnp.bfloat16
NT = (((1,), (1,)), ((), ()))
NN = (((1,), (0,)), ((), ()))
TN = (((0,), (0,)), ((), ()))


def dot(a, b, dims):
    return lax.dot_general(a, b, dims, preferred_element_type=F32)


def exchange_kernel(
    C, S, T, RB, CB, tile, G,
    index, counts, tok, cot, gate_t, up_t, down_t,
    got_out, meta_out, gate_g, up_g, down_g,
    index_v, counts_v, meta, tiles_v, grads_v,
    meta_v, meta_s, blocks, pack, send_a, recv_a, X, P, Pb, recv_b, sums, acts, Q, send_c,
    m_send, m_recv, a_send, a_recv, b_send, b_recv, c_send, c_recv, in_sem, out_sem, local_sem,
    save_sem,
):
    N = C * T
    H, peers = N // G, C // G
    mc, mr = lax.axis_index("col"), lax.axis_index("row")
    partner = 1 - mr
    index_copy = pltpu.make_async_copy(index, index_v, in_sem.at[3])
    counts_copy = pltpu.make_async_copy(counts, counts_v, in_sem.at[4])
    tile_copies = [
        pltpu.make_async_copy(ref, tiles_v.at[m], in_sem.at[m])
        for m, ref in enumerate((gate_t, up_t, down_t))
    ]
    grad_copies = [
        pltpu.make_async_copy(grads_v.at[m], ref, out_sem.at[m])
        for m, ref in enumerate((gate_g, up_g, down_g))
    ]
    index_copy.start()
    counts_copy.start()
    for copy in tile_copies:
        copy.start()

    barrier = pltpu.get_barrier_semaphore()

    def greet(k, _):
        pl.semaphore_signal(barrier, inc=1, device_id={"col": lax.rem(mc + k, C)}, device_id_type=MESH)
        return 0

    lax.fori_loop(1, C, greet, 0)
    pl.semaphore_signal(barrier, inc=1, device_id={"row": partner}, device_id_type=MESH)
    index_copy.wait()
    counts_copy.wait()
    meta[...] = jnp.zeros_like(meta)
    for m in range(3):
        meta[2 * m:2 * m + 2, 0:S] = index_v[m]
    meta[6:7, 0:3] = counts_v[0]
    pl.semaphore_wait(barrier, C)

    def meta_copy(k, owner, target):
        return pltpu.make_async_remote_copy(
            src_ref=meta, dst_ref=meta_v.at[owner], send_sem=m_send.at[k], recv_sem=m_recv.at[k],
            device_id={"col": target}, device_id_type=MESH,
        )

    def meta_row(owner):
        return pltpu.make_async_remote_copy(
            src_ref=meta, dst_ref=meta_v.at[C + owner], send_sem=m_send.at[0], recv_sem=m_recv.at[0],
            device_id={"row": partner}, device_id_type=MESH,
        )

    def meta_start(k, _):
        meta_copy(k, mc, lax.rem(mc + k, C)).start()
        return 0

    lax.fori_loop(1, C, meta_start, 0)
    meta_row(mr).start()
    meta_v[mc] = meta[...]
    meta_v[C + mr] = meta[...]
    for b in range(RB):
        blocks[b, 0:T, :] = tok[:, b * tile:(b + 1) * tile].astype(F32)
        blocks[RB + b, 0:T, :] = cot[:, b * tile:(b + 1) * tile].astype(F32)
    pack[...] = jnp.zeros_like(pack)

    def meta_wait(k, _):
        meta_copy(k, lax.rem(mc - k + C, C), lax.rem(mc + k, C)).wait()
        return 0

    lax.fori_loop(1, C, meta_wait, 0)
    meta_row(partner).wait()
    to_smem = pltpu.make_async_copy(meta_v, meta_s, local_sem)
    to_smem.start()
    to_smem.wait()
    meta_save = pltpu.make_async_copy(meta_v, meta_out, save_sem)
    meta_save.start()

    def a_copy(k, owner, target):
        return pltpu.make_async_remote_copy(
            src_ref=send_a.at[k], dst_ref=recv_a.at[owner], send_sem=a_send.at[k], recv_sem=a_recv.at[k],
            device_id={"col": target}, device_id_type=MESH,
        )

    def pick_for(dest):
        for s in range(3 * S):
            m = s // S
            side, base = (1, RB) if m == 2 else (0, 0)
            b = meta_s[dest, 2 * m + side, s % S] + base
            pack[s * T:(s + 1) * T, :] = blocks[b, 0:T, :]

    def a_start(k, _):
        dest = lax.rem(mc + k, C)
        pick_for(dest)
        send_a[k] = pack[...].astype(BF16)
        a_copy(k, mc, dest).start()
        return 0

    lax.fori_loop(1, C, a_start, 0)
    pick_for(mc)
    for s in range(3 * S):
        X[s, 0:T, :] = pack[s * T:(s + 1) * T, :]

    def a_wait(k, _):
        src = lax.rem(mc - k + C, C)
        a_copy(k, src, lax.rem(mc + k, C)).wait()
        pack[...] = recv_a[src].astype(F32)
        for s in range(3 * S):
            X[s, pl.ds(k * T, T), :] = pack[s * T:(s + 1) * T, :]
        return 0

    def live(m, s):
        return s < meta_s[mc, 6, m]

    def b_copy(g, m):
        return pltpu.make_async_remote_copy(
            src_ref=Pb.at[g, m], dst_ref=recv_b.at[g, m],
            send_sem=b_send.at[g, m], recv_sem=b_recv.at[g, m],
            device_id={"row": partner}, device_id_type=MESH,
        )

    def c_copy(k, owner, target):
        return pltpu.make_async_remote_copy(
            src_ref=send_c.at[k], dst_ref=got_out.at[owner], send_sem=c_send.at[k], recv_sem=c_recv.at[k],
            device_id={"col": target}, device_id_type=MESH,
        )

    def c_start(k, _):
        for s in range(3 * S):
            pack[s * T:(s + 1) * T, :] = Q[s, pl.ds(k * T, T), :]
        send_c[k] = pack[...].astype(BF16)
        c_copy(k, mc, lax.rem(mc - k + C, C)).start()
        return 0

    def forward(g):
        rows = slice(g * H, (g + 1) * H)
        lax.fori_loop(max(1, g * peers), (g + 1) * peers, a_wait, 0)
        if g == 0:
            for copy in tile_copies:
                copy.wait()
        for m in range(3):
            for s in range(S):
                part = dot(X[m * S + s, rows, :].astype(BF16), tiles_v[m, s], NT if m == 2 else NN)
                part = jnp.where(live(m, s), part, 0.0)
                P[m * S + s, rows, :] = part
                Pb[g, m, s, 0:H, :] = part.astype(BF16)
            b_copy(g, m).start()

        def place(j, _):
            for m in range(3):
                side = 0 if m == 2 else 1
                total = jnp.zeros((H, tile), F32)
                for s in range(S):
                    mine = meta_s[mc, 2 * m + side, s] == j
                    total = total + jnp.where(mine, P[m * S + s, rows, :], 0.0)
                sums[m, j, rows, :] = total
            return 0

        lax.fori_loop(0, CB, place, 0)

    def backward(g):
        rows = slice(g * H, (g + 1) * H)
        for m in range(3):
            b_copy(g, m).wait()

        def activate(j, _):
            whole = []
            for m in range(3):
                side = 0 if m == 2 else 1
                total = sums[m, j, rows, :]
                for s in range(S):
                    theirs = meta_s[C + partner, 2 * m + side, s] == j
                    total = total + jnp.where(theirs, recv_b[g, m, s, 0:H, :].astype(F32), 0.0)
                whole.append(total)
            gate, up, hg = whole
            sg = jax.nn.sigmoid(gate)
            active = gate * sg
            acts[0, j, rows, :] = hg * up * sg * (1.0 + gate * (1.0 - sg))
            acts[1, j, rows, :] = hg * active
            acts[2, j, rows, :] = active * up
            return 0

        lax.fori_loop(0, CB, activate, 0)
        for m in range(3):
            for s in range(S):
                j = meta_s[mc, 2 * m + (0 if m == 2 else 1), s]
                part = dot(acts[m, j, rows, :].astype(BF16), tiles_v[m, s], NN if m == 2 else NT)
                Q[m * S + s, rows, :] = jnp.where(live(m, s), part, 0.0)
        lax.fori_loop(max(1, g * peers), (g + 1) * peers, c_start, 0)

    for g in range(G):
        forward(g)
        if g >= 1:
            backward(g - 1)
    backward(G - 1)

    for s in range(3 * S):
        pack[s * T:(s + 1) * T, :] = Q[s, 0:T, :]
    send_c[0] = pack[...].astype(BF16)
    own_copy = pltpu.make_async_copy(send_c.at[0], got_out.at[mc], local_sem)
    own_copy.start()

    for m in range(3):
        for s in range(S):
            j = meta_s[mc, 2 * m + (0 if m == 2 else 1), s]
            x = X[m * S + s].astype(BF16)
            act = acts[m, j].astype(BF16)
            part = dot(act, x, TN) if m == 2 else dot(x, act, TN)
            grads_v[m, s] = jnp.where(live(m, s), part, 0.0)
        grad_copies[m].start()

    def c_wait(k, _):
        src = lax.rem(mc + k, C)
        c_copy(k, src, lax.rem(mc - k + C, C)).wait()
        return 0

    lax.fori_loop(1, C, c_wait, 0)
    own_copy.wait()
    meta_save.wait()
    for copy in grad_copies:
        copy.wait()


def add_kernel(
    C, S, T, RB, tile, meta, got, gate_in, up_in, down_in,
    out, ingrad, gate_g, up_g, down_g, total, pack, held, load_sem, store_sem,
):
    loads = [
        pltpu.make_async_copy(src, held.at[m], load_sem.at[m])
        for m, src in enumerate((gate_in, up_in, down_in))
    ]
    stores = [
        pltpu.make_async_copy(held.at[m], dst, store_sem.at[m])
        for m, dst in enumerate((gate_g, up_g, down_g))
    ]
    for copy in loads:
        copy.start()
    total[...] = jnp.zeros_like(total)

    def add(c, _):
        pack[...] = got[c].astype(F32)
        for s in range(3 * S):
            m = s // S
            side, base = (1, RB) if m == 2 else (0, 0)
            b = meta[c, 2 * m + side, s % S] + base
            total[b, 0:T, :] += pack[s * T:(s + 1) * T, :]
        return 0

    lax.fori_loop(0, C, add, 0)
    for load, store in zip(loads, stores):
        load.wait()
        store.start()
    for b in range(RB):
        ingrad[:, b * tile:(b + 1) * tile] = total[b, 0:T, :].astype(BF16)
        out[:, b * tile:(b + 1) * tile] = total[RB + b, 0:T, :].astype(BF16)
    for store in stores:
        store.wait()


def sparse_body(tokens, cotangent, gate_tiles, up_tiles, down_tiles, tile_index, tile_counts):
    C, R = lax.axis_size("col"), lax.axis_size("row")
    T, width = tokens.shape
    S, tile = gate_tiles.shape[0], gate_tiles.shape[-1]
    RB, CB = width // tile, FF // C // tile
    N = C * T
    rows = -(-3 * S * T // 16) * 16
    pad_t = -(-T // 8) * 8
    G = max(g for g in (1, 2) if C % g == 0 and C // g * T % 8 == 0)
    padded = -(-(N // G) // 16) * 16
    meta_rows = 8
    index, counts = tile_index.transpose(0, 2, 1), tile_counts.transpose(1, 2, 0)
    V, M = pltpu.VMEM, pltpu.SemaphoreType.DMA
    vspec = pl.BlockSpec(memory_space=pltpu.VMEM)
    hbm = pl.BlockSpec(memory_space=pltpu.HBM)
    sd = jax.ShapeDtypeStruct
    got, metas, gate_grad, up_grad, down_grad = pl.pallas_call(
        functools.partial(exchange_kernel, C, S, T, RB, CB, tile, G),
        out_shape=[sd((C, rows, tile), BF16), sd((C + R, meta_rows, 128), jnp.int32)]
        + [sd((S, tile, tile), F32)] * 3,
        in_specs=[hbm] * 2 + [vspec] * 2 + [hbm] * 3,
        out_specs=[hbm] * 5,
        scratch_shapes=[
            V(index.shape, jnp.int32),
            V(counts.shape, jnp.int32),
            V((meta_rows, 128), jnp.int32),
            V((3, S, tile, tile), BF16),
            V((3, S, tile, tile), F32),
            V((C + R, meta_rows, 128), jnp.int32),
            pltpu.SMEM((C + R, meta_rows, 128), jnp.int32),
            V((2 * RB, pad_t, tile), F32),
            V((rows, tile), F32),
            V((C, rows, tile), BF16),
            V((C, rows, tile), BF16),
            V((3 * S, N, tile), F32),
            V((3 * S, N, tile), F32),
            V((G, 3, S, padded, tile), BF16),
            V((G, 3, S, padded, tile), BF16),
            V((3, CB, N, tile), F32),
            V((3, CB, N, tile), F32),
            V((3 * S, N, tile), F32),
            V((C, rows, tile), BF16),
            M((C,)), M((C,)), M((C,)), M((C,)), M((G, 3)), M((G, 3)), M((C,)), M((C,)),
            M((5,)), M((3,)), M, M,
        ],
        compiler_params=pltpu.CompilerParams(
            collective_id=0, has_side_effects=True, vmem_limit_bytes=60 * 1024 * 1024
        ),
        name="exchange",
    )(index, counts, tokens, cotangent, gate_tiles, up_tiles, down_tiles)
    return pl.pallas_call(
        functools.partial(add_kernel, C, S, T, RB, tile),
        out_shape=[sd((T, width), BF16)] * 2 + [sd((S, tile, tile), F32)] * 3,
        in_specs=[pl.BlockSpec(memory_space=pltpu.SMEM), vspec] + [hbm] * 3,
        out_specs=[vspec] * 2 + [hbm] * 3,
        scratch_shapes=[
            V((2 * RB, pad_t, tile), F32), V((rows, tile), F32),
            V((3, S, tile, tile), F32), M((3,)), M((3,)),
        ],
        compiler_params=pltpu.CompilerParams(vmem_limit_bytes=60 * 1024 * 1024),
        name="add_slots",
    )(metas, got, gate_grad, up_grad, down_grad)


def solution(mesh):
    body = sparse_body if mesh.shape["row"] == 2 else dense_body
    return jax.shard_map(
        body,
        mesh=mesh,
        in_specs=(
            P("col", "row"),
            P("col", "row"),
            P("row", "col", None),
            P("row", "col", None),
            P("row", "col", None),
            P(None, "row", "col"),
            P(None, "row", "col"),
        ),
        out_specs=(
            P("col", "row"),
            P("col", "row"),
            P("row", "col", None),
            P("row", "col", None),
            P("row", "col", None),
        ),
        check_vma=False,
    )
```

```python
import functools

import jax
import jax.numpy as jnp
from jax import lax
from jax.experimental import pallas as pl
from jax.experimental.pallas import tpu as pltpu
from jax.sharding import PartitionSpec as P

FF = 16384


def pick_blocks(data_rows, block_ids, tile_size):
    token_count = data_rows.shape[0]
    block_count = data_rows.shape[1] // tile_size
    split_rows = data_rows.reshape(token_count, block_count, tile_size)
    select = (block_ids[:, None] == jnp.arange(block_count)[None, :]).astype(jnp.bfloat16)
    picked = jnp.einsum("tbk,sb->tsk", split_rows, select, preferred_element_type=jnp.float32)
    return picked.astype(jnp.bfloat16)


def place_blocks(products, block_ids, live_mask, block_count):
    select = ((block_ids[:, None] == jnp.arange(block_count)[None, :]) & live_mask[:, None]).astype(
        jnp.float32
    )
    placed = jnp.einsum("tsn,sc->tcn", products, select, precision=lax.Precision.HIGHEST)
    return placed.reshape(products.shape[0], block_count * products.shape[2])


def sparse_apply(data_rows, tiles, in_ids, out_ids, live_mask, out_count):
    picked = pick_blocks(data_rows, in_ids, tiles.shape[-1])
    products = jnp.einsum("tsk,skn->tsn", picked, tiles, preferred_element_type=jnp.float32)
    return place_blocks(products, out_ids, live_mask, out_count)


def sparse_apply_back(data_rows, tiles, in_ids, out_ids, live_mask, out_count):
    picked = pick_blocks(data_rows, in_ids, tiles.shape[-1])
    products = jnp.einsum("tsn,skn->tsk", picked, tiles, preferred_element_type=jnp.float32)
    return place_blocks(products, out_ids, live_mask, out_count)


def tile_grads(left_rows, right_rows, left_ids, right_ids, live_mask, tile_size):
    left_picked = pick_blocks(left_rows, left_ids, tile_size)
    right_picked = pick_blocks(right_rows, right_ids, tile_size)
    gradient = jnp.einsum(
        "tsk,tsn->skn", left_picked, right_picked, preferred_element_type=jnp.float32
    )
    return jnp.where(live_mask[:, None, None], gradient, jnp.zeros_like(gradient))


def gated_units(gate_sum, up_sum, hidden_grad):
    sigmoid_gate = jax.nn.sigmoid(gate_sum)
    active = gate_sum * sigmoid_gate
    hidden = (active * up_sum).astype(jnp.bfloat16)
    gate_act = (
        hidden_grad * up_sum * sigmoid_gate * (1.0 + gate_sum * (1.0 - sigmoid_gate))
    ).astype(jnp.bfloat16)
    up_act = (hidden_grad * active).astype(jnp.bfloat16)
    return (hidden, gate_act, up_act)


def dense_body(tokens, cotangent, gate_tiles, up_tiles, down_tiles, tile_index, tile_counts):
    tile_size = gate_tiles.shape[-1]
    row_blocks = tokens.shape[1] // tile_size
    col_blocks = FF // lax.axis_size("col") // tile_size
    slot_ids = jnp.arange(gate_tiles.shape[0])
    gate_live = slot_ids < tile_counts[0, 0, 0]
    up_live = slot_ids < tile_counts[1, 0, 0]
    down_live = slot_ids < tile_counts[2, 0, 0]
    gate_in, gate_out = (tile_index[0, :, 0], tile_index[0, :, 1])
    up_in, up_out = (tile_index[1, :, 0], tile_index[1, :, 1])
    down_in, down_out = (tile_index[2, :, 0], tile_index[2, :, 1])
    whole_tokens, whole_cotangent = (
        lax.all_gather(tokens, "col", axis=0, tiled=True),
        lax.all_gather(cotangent, "col", axis=0, tiled=True),
    )
    gate_part = sparse_apply(whole_tokens, gate_tiles, gate_in, gate_out, gate_live, col_blocks)
    up_part = sparse_apply(whole_tokens, up_tiles, up_in, up_out, up_live, col_blocks)
    grad_part = sparse_apply_back(
        whole_cotangent, down_tiles, down_out, down_in, down_live, col_blocks
    )
    gate_sum, up_sum, hidden_grad = (
        lax.psum_scatter(gate_part, "row", scatter_dimension=0, tiled=True),
        lax.psum_scatter(up_part, "row", scatter_dimension=0, tiled=True),
        lax.psum_scatter(grad_part, "row", scatter_dimension=0, tiled=True),
    )
    hidden, gate_act, up_act = gated_units(gate_sum, up_sum, hidden_grad)
    hidden_all, gate_all, up_all = (
        lax.all_gather(hidden, "row", axis=0, tiled=True),
        lax.all_gather(gate_act, "row", axis=0, tiled=True),
        lax.all_gather(up_act, "row", axis=0, tiled=True),
    )
    output_part = sparse_apply(hidden_all, down_tiles, down_in, down_out, down_live, row_blocks)
    input_part = sparse_apply_back(gate_all, gate_tiles, gate_out, gate_in, gate_live, row_blocks)
    input_part = input_part + sparse_apply_back(
        up_all, up_tiles, up_out, up_in, up_live, row_blocks
    )
    output_sum, input_sum = (
        lax.psum_scatter(output_part, "col", scatter_dimension=0, tiled=True),
        lax.psum_scatter(input_part, "col", scatter_dimension=0, tiled=True),
    )
    output = output_sum.astype(jnp.bfloat16)
    input_grad = input_sum.astype(jnp.bfloat16)
    gate_grad = tile_grads(whole_tokens, gate_all, gate_in, gate_out, gate_live, tile_size)
    up_grad = tile_grads(whole_tokens, up_all, up_in, up_out, up_live, tile_size)
    down_grad = tile_grads(hidden_all, whole_cotangent, down_in, down_out, down_live, tile_size)
    return (output, input_grad, gate_grad, up_grad, down_grad)


MESH = pl.DeviceIdType.MESH
F32 = jnp.float32
BF16 = jnp.bfloat16
NT = (((1,), (1,)), ((), ()))
NN = (((1,), (0,)), ((), ()))
TN = (((0,), (0,)), ((), ()))


def dot(a, b, dims):
    return lax.dot_general(a, b, dims, preferred_element_type=F32)


def exchange_kernel(
    C, S, T, RB, CB, tile, G,
    index, counts, tok, cot, gate_t, up_t, down_t,
    got_out, meta_out, gate_g, up_g, down_g,
    index_v, counts_v, meta, tiles_v, grads_v,
    meta_v, meta_s, blocks, pack, send_a, recv_a, X, P, Pb, recv_b, sums, acts, Q, send_c,
    m_send, m_recv, a_send, a_recv, b_send, b_recv, c_send, c_recv, in_sem, out_sem, local_sem,
    save_sem,
):
    N = C * T
    H, peers = N // G, C // G
    mc, mr = lax.axis_index("col"), lax.axis_index("row")
    partner = 1 - mr
    index_copy = pltpu.make_async_copy(index, index_v, in_sem.at[3])
    counts_copy = pltpu.make_async_copy(counts, counts_v, in_sem.at[4])
    tile_copies = [
        pltpu.make_async_copy(ref, tiles_v.at[m], in_sem.at[m])
        for m, ref in enumerate((gate_t, up_t, down_t))
    ]
    grad_copies = [
        pltpu.make_async_copy(grads_v.at[m], ref, out_sem.at[m])
        for m, ref in enumerate((gate_g, up_g, down_g))
    ]
    index_copy.start()
    counts_copy.start()
    for copy in tile_copies:
        copy.start()

    barrier = pltpu.get_barrier_semaphore()

    def greet(k, _):
        pl.semaphore_signal(barrier, inc=1, device_id={"col": lax.rem(mc + k, C)}, device_id_type=MESH)
        return 0

    lax.fori_loop(1, C, greet, 0)
    pl.semaphore_signal(barrier, inc=1, device_id={"row": partner}, device_id_type=MESH)
    index_copy.wait()
    counts_copy.wait()
    meta[...] = jnp.zeros_like(meta)
    for m in range(3):
        meta[2 * m:2 * m + 2, 0:S] = index_v[m]
    meta[6:7, 0:3] = counts_v[0]
    pl.semaphore_wait(barrier, C)

    def meta_copy(k, owner, target):
        return pltpu.make_async_remote_copy(
            src_ref=meta, dst_ref=meta_v.at[owner], send_sem=m_send.at[k], recv_sem=m_recv.at[k],
            device_id={"col": target}, device_id_type=MESH,
        )

    def meta_row(owner):
        return pltpu.make_async_remote_copy(
            src_ref=meta, dst_ref=meta_v.at[C + owner], send_sem=m_send.at[0], recv_sem=m_recv.at[0],
            device_id={"row": partner}, device_id_type=MESH,
        )

    def meta_start(k, _):
        meta_copy(k, mc, lax.rem(mc + k, C)).start()
        return 0

    lax.fori_loop(1, C, meta_start, 0)
    meta_row(mr).start()
    meta_v[mc] = meta[...]
    meta_v[C + mr] = meta[...]
    for b in range(RB):
        blocks[b, 0:T, :] = tok[:, b * tile:(b + 1) * tile].astype(F32)
        blocks[RB + b, 0:T, :] = cot[:, b * tile:(b + 1) * tile].astype(F32)
    pack[...] = jnp.zeros_like(pack)

    def meta_wait(k, _):
        meta_copy(k, lax.rem(mc - k + C, C), lax.rem(mc + k, C)).wait()
        return 0

    lax.fori_loop(1, C, meta_wait, 0)
    meta_row(partner).wait()
    to_smem = pltpu.make_async_copy(meta_v, meta_s, local_sem)
    to_smem.start()
    to_smem.wait()
    meta_save = pltpu.make_async_copy(meta_v, meta_out, save_sem)
    meta_save.start()

    def a_copy(k, owner, target):
        return pltpu.make_async_remote_copy(
            src_ref=send_a.at[k], dst_ref=recv_a.at[owner], send_sem=a_send.at[k], recv_sem=a_recv.at[k],
            device_id={"col": target}, device_id_type=MESH,
        )

    def pick_for(dest):
        for s in range(3 * S):
            m = s // S
            side, base = (1, RB) if m == 2 else (0, 0)
            b = meta_s[dest, 2 * m + side, s % S] + base
            pack[s * T:(s + 1) * T, :] = blocks[b, 0:T, :]

    def a_start(k, _):
        dest = lax.rem(mc + k, C)
        pick_for(dest)
        send_a[k] = pack[...].astype(BF16)
        a_copy(k, mc, dest).start()
        return 0

    lax.fori_loop(1, C, a_start, 0)
    pick_for(mc)
    for s in range(3 * S):
        X[s, 0:T, :] = pack[s * T:(s + 1) * T, :]

    def a_wait(k, _):
        src = lax.rem(mc - k + C, C)
        a_copy(k, src, lax.rem(mc + k, C)).wait()
        pack[...] = recv_a[src].astype(F32)
        for s in range(3 * S):
            X[s, pl.ds(k * T, T), :] = pack[s * T:(s + 1) * T, :]
        return 0

    def live(m, s):
        return s < meta_s[mc, 6, m]

    def b_copy(g, m):
        return pltpu.make_async_remote_copy(
            src_ref=Pb.at[g, m], dst_ref=recv_b.at[g, m],
            send_sem=b_send.at[g, m], recv_sem=b_recv.at[g, m],
            device_id={"row": partner}, device_id_type=MESH,
        )

    def c_copy(k, owner, target):
        return pltpu.make_async_remote_copy(
            src_ref=send_c.at[k], dst_ref=got_out.at[owner], send_sem=c_send.at[k], recv_sem=c_recv.at[k],
            device_id={"col": target}, device_id_type=MESH,
        )

    def c_start(k, _):
        for s in range(3 * S):
            pack[s * T:(s + 1) * T, :] = Q[s, pl.ds(k * T, T), :]
        send_c[k] = pack[...].astype(BF16)
        c_copy(k, mc, lax.rem(mc - k + C, C)).start()
        return 0

    def forward(g):
        rows = slice(g * H, (g + 1) * H)
        lax.fori_loop(max(1, g * peers), (g + 1) * peers, a_wait, 0)
        if g == 0:
            for copy in tile_copies:
                copy.wait()
        for m in range(3):
            for s in range(S):
                part = dot(X[m * S + s, rows, :].astype(BF16), tiles_v[m, s], NT if m == 2 else NN)
                part = jnp.where(live(m, s), part, 0.0)
                P[m * S + s, rows, :] = part
                Pb[g, m, s, 0:H, :] = part.astype(BF16)
            b_copy(g, m).start()

        def place(j, _):
            for m in range(3):
                side = 0 if m == 2 else 1
                total = jnp.zeros((H, tile), F32)
                for s in range(S):
                    mine = meta_s[mc, 2 * m + side, s] == j
                    total = total + jnp.where(mine, P[m * S + s, rows, :], 0.0)
                sums[m, j, rows, :] = total
            return 0

        lax.fori_loop(0, CB, place, 0)

    def backward(g):
        rows = slice(g * H, (g + 1) * H)
        for m in range(3):
            b_copy(g, m).wait()

        def activate(j, _):
            whole = []
            for m in range(3):
                side = 0 if m == 2 else 1
                total = sums[m, j, rows, :]
                for s in range(S):
                    theirs = meta_s[C + partner, 2 * m + side, s] == j
                    total = total + jnp.where(theirs, recv_b[g, m, s, 0:H, :].astype(F32), 0.0)
                whole.append(total)
            gate, up, hg = whole
            sg = jax.nn.sigmoid(gate)
            active = gate * sg
            acts[0, j, rows, :] = hg * up * sg * (1.0 + gate * (1.0 - sg))
            acts[1, j, rows, :] = hg * active
            acts[2, j, rows, :] = active * up
            return 0

        lax.fori_loop(0, CB, activate, 0)
        for m in range(3):
            for s in range(S):
                j = meta_s[mc, 2 * m + (0 if m == 2 else 1), s]
                part = dot(acts[m, j, rows, :].astype(BF16), tiles_v[m, s], NN if m == 2 else NT)
                Q[m * S + s, rows, :] = jnp.where(live(m, s), part, 0.0)
        lax.fori_loop(max(1, g * peers), (g + 1) * peers, c_start, 0)

    for g in range(G):
        forward(g)
        if g >= 1:
            backward(g - 1)
    backward(G - 1)

    for s in range(3 * S):
        pack[s * T:(s + 1) * T, :] = Q[s, 0:T, :]
    send_c[0] = pack[...].astype(BF16)
    own_copy = pltpu.make_async_copy(send_c.at[0], got_out.at[mc], local_sem)
    own_copy.start()

    for m in range(3):
        for s in range(S):
            j = meta_s[mc, 2 * m + (0 if m == 2 else 1), s]
            x = X[m * S + s].astype(BF16)
            act = acts[m, j].astype(BF16)
            part = dot(act, x, TN) if m == 2 else dot(x, act, TN)
            grads_v[m, s] = jnp.where(live(m, s), part, 0.0)
        grad_copies[m].start()

    def c_wait(k, _):
        src = lax.rem(mc + k, C)
        c_copy(k, src, lax.rem(mc - k + C, C)).wait()
        return 0

    lax.fori_loop(1, C, c_wait, 0)
    own_copy.wait()
    meta_save.wait()
    for copy in grad_copies:
        copy.wait()


def add_kernel(
    C, S, T, RB, tile, meta, got, gate_in, up_in, down_in,
    out, ingrad, gate_g, up_g, down_g, total, pack, held, load_sem, store_sem,
):
    loads = [
        pltpu.make_async_copy(src, held.at[m], load_sem.at[m])
        for m, src in enumerate((gate_in, up_in, down_in))
    ]
    stores = [
        pltpu.make_async_copy(held.at[m], dst, store_sem.at[m])
        for m, dst in enumerate((gate_g, up_g, down_g))
    ]
    for copy in loads:
        copy.start()
    total[...] = jnp.zeros_like(total)

    def add(c, _):
        pack[...] = got[c].astype(F32)
        for s in range(3 * S):
            m = s // S
            side, base = (1, RB) if m == 2 else (0, 0)
            b = meta[c, 2 * m + side, s % S] + base
            total[b, 0:T, :] += pack[s * T:(s + 1) * T, :]
        return 0

    lax.fori_loop(0, C, add, 0, unroll=2)
    for load, store in zip(loads, stores):
        load.wait()
        store.start()
    for b in range(RB):
        ingrad[:, b * tile:(b + 1) * tile] = total[b, 0:T, :].astype(BF16)
        out[:, b * tile:(b + 1) * tile] = total[RB + b, 0:T, :].astype(BF16)
    for store in stores:
        store.wait()


def sparse_body(tokens, cotangent, gate_tiles, up_tiles, down_tiles, tile_index, tile_counts):
    C, R = lax.axis_size("col"), lax.axis_size("row")
    T, width = tokens.shape
    S, tile = gate_tiles.shape[0], gate_tiles.shape[-1]
    RB, CB = width // tile, FF // C // tile
    N = C * T
    rows = -(-3 * S * T // 16) * 16
    pad_t = -(-T // 8) * 8
    G = max(g for g in (1, 2, 4) if C % g == 0 and C // g * T % 8 == 0)
    padded = -(-(N // G) // 16) * 16
    meta_rows = 8
    index, counts = tile_index.transpose(0, 2, 1), tile_counts.transpose(1, 2, 0)
    V, M = pltpu.VMEM, pltpu.SemaphoreType.DMA
    vspec = pl.BlockSpec(memory_space=pltpu.VMEM)
    hbm = pl.BlockSpec(memory_space=pltpu.HBM)
    sd = jax.ShapeDtypeStruct
    got, metas, gate_grad, up_grad, down_grad = pl.pallas_call(
        functools.partial(exchange_kernel, C, S, T, RB, CB, tile, G),
        out_shape=[sd((C, rows, tile), BF16), sd((C + R, meta_rows, 128), jnp.int32)]
        + [sd((S, tile, tile), F32)] * 3,
        in_specs=[hbm] * 2 + [vspec] * 2 + [hbm] * 3,
        out_specs=[hbm] * 5,
        scratch_shapes=[
            V(index.shape, jnp.int32),
            V(counts.shape, jnp.int32),
            V((meta_rows, 128), jnp.int32),
            V((3, S, tile, tile), BF16),
            V((3, S, tile, tile), F32),
            V((C + R, meta_rows, 128), jnp.int32),
            pltpu.SMEM((C + R, meta_rows, 128), jnp.int32),
            V((2 * RB, pad_t, tile), F32),
            V((rows, tile), F32),
            V((C, rows, tile), BF16),
            V((C, rows, tile), BF16),
            V((3 * S, N, tile), F32),
            V((3 * S, N, tile), F32),
            V((G, 3, S, padded, tile), BF16),
            V((G, 3, S, padded, tile), BF16),
            V((3, CB, N, tile), F32),
            V((3, CB, N, tile), F32),
            V((3 * S, N, tile), F32),
            V((C, rows, tile), BF16),
            M((C,)), M((C,)), M((C,)), M((C,)), M((G, 3)), M((G, 3)), M((C,)), M((C,)),
            M((5,)), M((3,)), M, M,
        ],
        compiler_params=pltpu.CompilerParams(
            collective_id=0, has_side_effects=True, vmem_limit_bytes=60 * 1024 * 1024
        ),
        name="exchange",
    )(index, counts, tokens, cotangent, gate_tiles, up_tiles, down_tiles)
    return pl.pallas_call(
        functools.partial(add_kernel, C, S, T, RB, tile),
        out_shape=[sd((T, width), BF16)] * 2 + [sd((S, tile, tile), F32)] * 3,
        in_specs=[pl.BlockSpec(memory_space=pltpu.SMEM), vspec] + [hbm] * 3,
        out_specs=[vspec] * 2 + [hbm] * 3,
        scratch_shapes=[
            V((2 * RB, pad_t, tile), F32), V((rows, tile), F32),
            V((3, S, tile, tile), F32), M((3,)), M((3,)),
        ],
        compiler_params=pltpu.CompilerParams(vmem_limit_bytes=60 * 1024 * 1024),
        name="add_slots",
    )(metas, got, gate_grad, up_grad, down_grad)


def solution(mesh):
    body = sparse_body if mesh.shape["row"] == 2 else dense_body
    return jax.shard_map(
        body,
        mesh=mesh,
        in_specs=(
            P("col", "row"),
            P("col", "row"),
            P("row", "col", None),
            P("row", "col", None),
            P("row", "col", None),
            P(None, "row", "col"),
            P(None, "row", "col"),
        ),
        out_specs=(
            P("col", "row"),
            P("col", "row"),
            P("row", "col", None),
            P("row", "col", None),
            P("row", "col", None),
        ),
        check_vma=False,
    )
```
